128 devices in a mesh: ulysses: 4 (over z_lo, core), context: 32 (over x, y, z_hi).
Axes of the slice: x: 4, y: 4, z: 4 (z_hi: 2, z_lo: 2; z = z_hi * 2 + z_lo), core: 2. Of those that a mesh axis runs over, the one named last changes fastest.
Arguments:
- queries: bfloat16 [16384, 2048], P(('context', 'ulysses')), may hold values from -6 to 6
- key_rows: bfloat16 [16384, 2048], P(('context', 'ulysses')), may hold values from -6 to 6
- value_rows: bfloat16 [16384, 2048], P(('context', 'ulysses')), may hold values from -6 to 6
- grad_out: bfloat16 [16384, 2048], P(('context', 'ulysses')), may hold values from -6 to 6
Outputs:
- attended: bfloat16 [16384, 2048], P(('context', 'ulysses'))
- grad_queries: bfloat16 [16384, 2048], P(('context', 'ulysses'))
- grad_keys: bfloat16 [16384, 2048], P(('context', 'ulysses'))
- grad_values: bfloat16 [16384, 2048], P(('context', 'ulysses'))
The draws below stay inside these ranges and needn't reach their ends.
All inputs are finite; a program needn't handle non-finite values.
Results may differ from the reference program's by a relative error of at most 0.03.
Values may be sent and summed in bfloat16 or wider, within the bound.
A program may use at most 128 MiB of HBM per device.

```python
import jax
import jax.numpy as jnp
from jax import lax

HEADS = 16
HEAD_DIM = 128
D = 2048
BLOCK = 512
LEVELS = 5
TOKENS = 16384


def drawn_pair(key):
    base_key = jax.random.fold_in(key, 7)
    query_part = jnp.clip(jax.random.normal(jax.random.fold_in(base_key, 1), (TOKENS, D), jnp.float32), -6.0, 6.0)
    key_part = jnp.clip(jax.random.normal(jax.random.fold_in(base_key, 2), (TOKENS, D), jnp.float32), -6.0, 6.0)
    return (query_part, key_part)


def draw_queries(key, part):
    return drawn_pair(key)[0].astype(jnp.bfloat16)


def draw_key_rows(key, part):
    return drawn_pair(key)[1].astype(jnp.bfloat16)


def level_of(own_key, dims, shards, least, high):
    def one(axis_at, parts):
        draws = jax.random.uniform(jax.random.fold_in(jax.random.fold_in(own_key, 6), axis_at), (parts,), jnp.float32, least / len(shards), high / len(shards))
        return jnp.repeat(jnp.exp(draws), dims[axis_at] // parts).reshape((-1,) + (1,) * (len(dims) - axis_at - 1))

    level = one(*shards[0])
    for cut in shards[1:]:
        level = level * one(*cut)
    return level


def scatter_about(key, shape, spread, reach, split=(), kind=jnp.bfloat16):
    gain = level_of(key, shape, split, -0.22, 0.18) if split else 1.0
    drawn = jax.random.normal(key, shape, jnp.float32) * spread * gain
    return jnp.minimum(jnp.maximum(drawn, -reach), reach).astype(kind)


def setup_inputs(seed: int = 0) -> dict:
    seeds = jax.random.split(jax.random.key(seed), 5)
    return {
        "queries": draw_queries(jax.random.fold_in(seeds[4], 71), 0),
        "key_rows": draw_key_rows(jax.random.fold_in(seeds[4], 71), 0),
        "value_rows": scatter_about(seeds[2], (TOKENS, D), 1.0, 6.0, ((0, 128),)),
        "grad_out": scatter_about(seeds[3], (TOKENS, D), 1.0, 6.0, ((0, 128),)),
    }


def rounded_values(values_in):
    return lax.optimization_barrier(values_in.astype(jnp.bfloat16)).astype(jnp.float32)


def one_head(head_args, partner):
    query_h, key_h, value_h, grad_h = head_args
    softmax_scale = HEAD_DIM ** -0.5
    query_full = query_h.astype(jnp.float32)
    gradient_full = grad_h.astype(jnp.float32)
    key_groups = key_h[partner].astype(jnp.float32)
    value_groups = value_h[partner].astype(jnp.float32)
    logit_scores = jnp.einsum("hpe,hwye->hwpy", query_full, key_groups) * softmax_scale
    block_peak = jnp.max(logit_scores, axis=-1)
    shifted = jnp.exp(logit_scores - block_peak[..., None])
    block_total = jnp.sum(shifted, axis=-1)
    block_weights = rounded_values(shifted)
    block_out = jnp.einsum("bjqk,bjkd->bjqd", block_weights, value_groups)
    peak = jnp.max(block_peak, axis=1)
    factor = jnp.exp(block_peak - peak[:, None, :])
    norm = jnp.sum(factor * block_total, axis=1)
    attended = (jnp.sum(factor[..., None] * block_out, axis=1) / norm[..., None]).astype(jnp.bfloat16)
    log_norm = peak + jnp.log(norm)
    dot_term = jnp.sum(gradient_full * attended.astype(jnp.float32), axis=-1)
    probs = jnp.exp(logit_scores - log_norm[:, None, :, None])
    probabilities_reduced = rounded_values(probs)
    value_contributions = rounded_values(jnp.einsum("onhp,oha->onpa", probabilities_reduced, gradient_full))
    probability_gradient = jnp.einsum("hpe,hwye->hwpy", gradient_full, value_groups)
    score_gradient = rounded_values(probs * (probability_gradient - dot_term[:, None, :, None]) * softmax_scale)
    query_terms = rounded_values(jnp.einsum("bjqk,bjkd->bjqd", score_gradient, key_groups))
    key_contributions = rounded_values(jnp.einsum("onhp,oha->onpa", score_gradient, query_full))
    slot_index = jnp.arange(LEVELS + 1, dtype=jnp.int32)[None, :]
    grad_query = jnp.sum(query_terms, axis=1).astype(jnp.bfloat16)
    grad_key = jnp.sum(key_contributions[partner, slot_index], axis=1).astype(jnp.bfloat16)
    grad_value = jnp.sum(value_contributions[partner, slot_index], axis=1).astype(jnp.bfloat16)
    return attended, grad_query, grad_key, grad_value


def reference(queries, key_rows, value_rows, grad_out):
    nblocks = TOKENS // BLOCK

    def by_heads(array_in):
        return array_in.reshape(nblocks, BLOCK, HEADS, HEAD_DIM).transpose(2, 0, 1, 3)

    def by_tokens(array_in):
        return array_in.transpose(1, 2, 0, 3).reshape(TOKENS, D)

    block_ids = jnp.arange(nblocks, dtype=jnp.int32)
    distances = jnp.concatenate([jnp.zeros((1,), jnp.int32), jnp.left_shift(jnp.ones((LEVELS,), jnp.int32), jnp.arange(LEVELS, dtype=jnp.int32))])
    partner = jnp.bitwise_xor(block_ids[:, None], distances[None, :]).astype(jnp.int32)
    results = lax.map(lambda head_args: one_head(head_args, partner), (by_heads(queries), by_heads(key_rows), by_heads(value_rows), by_heads(grad_out)))
    return (by_tokens(results[0]), by_tokens(results[1]), by_tokens(results[2]), by_tokens(results[3]))
```

```python
import jax
import jax.numpy as jnp
from jax import lax
from jax.experimental import pallas as pl
from jax.experimental.pallas import tpu as pltpu
from jax.sharding import PartitionSpec as P

HEAD_DIM = 128
BLOCK = 512
ROWS = 128
F32 = jnp.float32
BF16 = jnp.bfloat16
SCALE = HEAD_DIM ** -0.5
EXP2_SCALE = SCALE * 1.4426950408889634
MESH = pl.DeviceIdType.MESH

KEY, VALUE, QUERY, GRAD = range(4)


def dot(a, b, ca, cb):
    return lax.dot_general(a, b, (((ca,), (cb,)), ((), ())), preferred_element_type=F32)


def kernel(
    q_in, k_in, v_in, g_in, out0, out1, out2, out3,
    kv, qg, qg_t, weights, peaks, run_peak, run_total, out_acc, query_acc, dots,
    acc, near, far_send, far_recv, near_send, near_recv, staged,
    in_send, in_recv, in_local, fwd_send, fwd_recv, far_ssem, far_rsem, near_ssem, near_rsem,
    out_send, out_recv, out_local,
):
    context = lax.axis_index("context")
    ulysses = lax.axis_index("ulysses")
    x = context // 8
    y = (context // 2) % 4
    z = (context % 2) * 2 + ulysses // 2
    core = ulysses % 2
    me = z * 2 + core

    def device(x, y, e):
        return {"context": x * 8 + y * 2 + e // 4, "ulysses": e % 4}

    def near_of(v):
        return v + 1 - 2 * (v % 2)

    def far_of(v):
        return 3 - v

    ring = [(me + k) % 8 for k in range(8)]
    near_device = [device(near_of(x), y, me), device(x, near_of(y), me)]
    far_device = [device(far_of(x), y, me), device(x, far_of(y), me)]

    def remote(src, dst, ssem, rsem, to):
        return pltpu.make_async_remote_copy(
            src_ref=src, dst_ref=dst, send_sem=ssem, recv_sem=rsem, device_id=to, device_id_type=MESH
        )

    inputs = {KEY: k_in, VALUE: v_in, QUERY: q_in, GRAD: g_in}

    def landing(array, h):
        return kv.at[0, array, h] if array < 2 else qg.at[array - 2, h]

    def columns(e, h):
        return pl.ds(pl.multiple_of(e * 256 + h * 128, 128), 128)

    def rows_of(e):
        return pl.ds(pl.multiple_of(e * ROWS, ROWS), ROWS)

    order = [(KEY, 0), (VALUE, 0), (QUERY, 0), (KEY, 1), (VALUE, 1), (GRAD, 0), (QUERY, 1), (GRAD, 1)]

    def local_in(array, h):
        return pltpu.make_async_copy(
            inputs[array].at[:, columns(me, h)], landing(array, h).at[rows_of(me)], in_local.at[array, h]
        )

    for array, h in order:
        local_in(array, h).start()

    barrier = pltpu.get_barrier_semaphore()
    partners = [device(x, y, ring[k]) for k in range(1, 8)] + near_device + far_device
    for partner in partners:
        pl.semaphore_signal(barrier, inc=1, device_id=partner, device_id_type=MESH)
    pl.semaphore_wait(barrier, len(partners))

    for array, h in order:
        for k in (4, 3, 5, 2, 6, 7, 1):
            remote(
                inputs[array].at[:, columns(ring[k], h)],
                landing(array, h).at[rows_of(me)],
                in_send.at[array, h],
                in_recv.at[array, h],
                device(x, y, ring[k]),
            ).start()

    def wait_in(array, h):
        local_in(array, h).wait()
        part = landing(array, h).at[pl.ds(0, 7 * ROWS)]
        pltpu.make_async_copy(part, part, in_recv.at[array, h]).wait()

    def block_rows(s):
        return pl.ds(pl.multiple_of(s * BLOCK, BLOCK), BLOCK)

    def hop(axis, hop_at, array, h, s):
        source = 0 if hop_at == 0 else 1 + 2 * axis
        return remote(
            kv.at[source, array, h, block_rows(s)],
            kv.at[1 + 2 * axis + hop_at, array, h, block_rows(s)],
            fwd_send.at[axis, hop_at, array, h, s],
            fwd_recv.at[axis, hop_at, array, h, s],
            near_device[axis] if hop_at == 0 else far_device[axis],
        )

    def start_near(array, h):
        for s in range(2):
            for axis in range(2):
                hop(axis, 0, array, h, s).start()

    def forward_far(array, h):
        for s in range(2):
            for axis in range(2):
                hop(axis, 0, array, h, s).wait_recv()
                hop(axis, 1, array, h, s).start()

    def wait_far(array, h):
        for s in range(2):
            for axis in range(2):
                hop(axis, 1, array, h, s).wait_recv()

    def turn(array, h):
        for s in range(2):
            qg_t[array - 2, h, s] = qg[array - 2, h, pl.ds(s * BLOCK, BLOCK), :].T

    def pair(j, h, s):
        source = 0 if j < 2 else j - 1
        rows = block_rows(1 - s if j == 1 else s)
        return kv[source, 0, h, rows, :], kv[source, 1, h, rows, :]

    def forward(j, h):
        def one(s, _):
            keys, values = pair(j, h, s)
            scores = dot(keys, qg_t[0, h, s], 1, 0)
            peak = jnp.max(scores, axis=0, keepdims=True)
            shifted = jnp.exp2((scores - peak) * EXP2_SCALE)
            total = jnp.sum(shifted, axis=0, keepdims=True)
            low = shifted.astype(BF16)
            weights[h, j, s] = low
            peaks[h, j, s] = peak
            part = dot(values, low, 0, 0)
            if j == 0:
                run_peak[h, s] = peak
                run_total[h, s] = total
                out_acc[h, s] = part
            else:
                old = run_peak[h, s]
                joined = jnp.maximum(old, peak)
                keep = jnp.exp2((old - joined) * EXP2_SCALE)
                fresh = jnp.exp2((peak - joined) * EXP2_SCALE)
                run_peak[h, s] = joined
                run_total[h, s] = run_total[h, s] * keep + total * fresh
                out_acc[h, s] = out_acc[h, s] * keep + part * fresh
            return 0

        lax.fori_loop(0, 2, one, 0)

    outs = [out0, out1, out2, out3]

    def out_copy(array, h, e):
        return remote(
            staged.at[array, h, rows_of(e)],
            outs[array].at[:, columns(me, h)],
            out_send.at[array, h],
            out_recv.at[array, h],
            device(x, y, e),
        )

    def out_keep(array, h):
        return pltpu.make_async_copy(
            staged.at[array, h, rows_of(me)], outs[array].at[:, columns(me, h)], out_local.at[array, h]
        )

    def send_out(array, h):
        for k in (4, 3, 5, 2, 6, 7, 1):
            out_copy(array, h, ring[k]).start()
        out_keep(array, h).start()

    def finish_forward(h):
        for s in range(2):
            attended = (out_acc[h, s] / run_total[h, s]).astype(BF16)
            dots[h, s] = jnp.sum(attended.astype(F32) * qg_t[1, h, s].astype(F32), axis=0, keepdims=True)
            staged[0, h, pl.ds(s * BLOCK, BLOCK)] = attended.T
        send_out(0, h)

    def far_copy(axis, array, h, s):
        return remote(
            far_send.at[axis, array, h, s], far_recv.at[axis, array, h, s],
            far_ssem.at[axis, array, h, s], far_rsem.at[axis, array, h, s], far_device[axis],
        )

    def near_copy(axis, array, h, s):
        return remote(
            near_send.at[axis, array, h, s], near_recv.at[axis, array, h, s],
            near_ssem.at[axis, array, h, s], near_rsem.at[axis, array, h, s], near_device[axis],
        )

    def backward(j, h, first=False):
        axis = (j - 2) // 2

        def one(s, _):
            keys, values = pair(j, h, s)
            low = weights[h, j, s]
            factor = jnp.exp2((peaks[h, j, s] - run_peak[h, s]) * EXP2_SCALE) / run_total[h, s]
            scaled = factor * SCALE
            grad_probs = dot(values, qg_t[1, h, s], 1, 0)
            grad_scores = (low.astype(F32) * (grad_probs - dots[h, s])).astype(BF16)
            query_part = dot(keys, grad_scores, 0, 0) * scaled
            if first:
                query_acc[h, s] = query_part
            else:
                query_acc[h, s] = query_acc[h, s] + query_part
            value_term = dot(low, (qg_t[1, h, s].astype(F32) * factor).astype(BF16), 1, 1)
            key_term = dot(grad_scores, (qg_t[0, h, s].astype(F32) * scaled).astype(BF16), 1, 1)
            if j == 0:
                acc[0, h, s] = key_term
                acc[1, h, s] = value_term
            elif j == 1:
                acc[0, h, 1 - s] = acc[0, h, 1 - s] + key_term
                acc[1, h, 1 - s] = acc[1, h, 1 - s] + value_term
            elif j % 2 == 0:
                near[axis, 0, h, s] = key_term
                near[axis, 1, h, s] = value_term
            else:
                far_send[axis, 0, h, s] = key_term.astype(BF16)
                far_send[axis, 1, h, s] = value_term.astype(BF16)
            return 0

        lax.fori_loop(0, 2, one, 0)
        if j >= 2 and j % 2 == 1:
            for s in range(2):
                for array in range(2):
                    far_copy(axis, array, h, s).start()

    def reduce_near(h):
        for s in range(2):
            for array in range(2):
                for axis in range(2):
                    far_copy(axis, array, h, s).wait_recv()
                    near_send[axis, array, h, s] = (
                        near[axis, array, h, s] + far_recv[axis, array, h, s].astype(F32)
                    ).astype(BF16)
                    near_copy(axis, array, h, s).start()

    def finish_queries(h):
        for s in range(2):
            staged[1, h, pl.ds(s * BLOCK, BLOCK)] = query_acc[h, s].astype(BF16).T
        send_out(1, h)

    def finish_keys(h):
        for array in range(2):
            for s in range(2):
                total = acc[array, h, s]
                for axis in range(2):
                    near_copy(axis, array, h, s).wait_recv()
                    total = total + near_recv[axis, array, h, s].astype(F32)
                staged[2 + array, h, pl.ds(s * BLOCK, BLOCK)] = total.astype(BF16)
            send_out(2 + array, h)

    wait_in(KEY, 0)
    start_near(KEY, 0)
    wait_in(VALUE, 0)
    start_near(VALUE, 0)
    wait_in(QUERY, 0)
    turn(QUERY, 0)
    forward(0, 0)
    forward_far(KEY, 0)
    forward(1, 0)
    wait_in(KEY, 1)
    start_near(KEY, 1)
    wait_in(VALUE, 1)
    start_near(VALUE, 1)
    forward_far(VALUE, 0)
    forward(2, 0)
    forward(4, 0)
    wait_in(GRAD, 0)
    turn(GRAD, 0)
    wait_in(QUERY, 1)
    turn(QUERY, 1)
    forward_far(KEY, 1)
    wait_far(KEY, 0)
    wait_far(VALUE, 0)
    forward(3, 0)
    forward(5, 0)
    finish_forward(0)
    backward(3, 0, first=True)
    forward_far(VALUE, 1)
    backward(5, 0)
    backward(2, 0)
    backward(4, 0)
    forward(0, 1)
    forward(1, 1)
    forward(2, 1)
    forward(4, 1)
    wait_in(GRAD, 1)
    turn(GRAD, 1)
    wait_far(KEY, 1)
    wait_far(VALUE, 1)
    forward(3, 1)
    forward(5, 1)
    finish_forward(1)
    backward(3, 1, first=True)
    backward(5, 1)
    reduce_near(0)
    backward(2, 1)
    backward(4, 1)
    backward(0, 0)
    backward(1, 0)
    finish_queries(0)
    backward(0, 1)
    backward(1, 1)
    finish_queries(1)
    finish_keys(0)
    reduce_near(1)
    finish_keys(1)

    for array in range(4):
        for h in range(2):
            part = landing(array, h).at[pl.ds(0, 7 * ROWS)]
            pltpu.make_async_copy(part, part, in_send.at[array, h]).wait()
    for array in range(2):
        for h in range(2):
            for s in range(2):
                for axis in range(2):
                    hop(axis, 0, array, h, s).wait_send()
                    hop(axis, 1, array, h, s).wait_send()
                    far_copy(axis, array, h, s).wait_send()
                    near_copy(axis, array, h, s).wait_send()
    for array in range(4):
        for h in range(2):
            out_keep(array, h).wait()
            part = staged.at[array, h, pl.ds(0, 7 * ROWS)]
            pltpu.make_async_copy(part, part, out_send.at[array, h]).wait()
            pltpu.make_async_copy(part, part, out_recv.at[array, h]).wait()


def body(queries, key_rows, value_rows, grad_out):
    dma = pltpu.SemaphoreType.DMA
    term = (2, 2, 2, 2, BLOCK, HEAD_DIM)
    shape = jax.ShapeDtypeStruct(queries.shape, BF16)
    return pl.pallas_call(
        kernel,
        out_shape=[shape] * 4,
        in_specs=[pl.BlockSpec(memory_space=pl.ANY)] * 4,
        out_specs=[pl.BlockSpec(memory_space=pl.ANY)] * 4,
        scratch_shapes=[
            pltpu.VMEM((5, 2, 2, 2 * BLOCK, HEAD_DIM), BF16),
            pltpu.VMEM((2, 2, 2 * BLOCK, HEAD_DIM), BF16),
            pltpu.VMEM((2, 2, 2, HEAD_DIM, BLOCK), BF16),
            pltpu.VMEM((2, 6, 2, BLOCK, BLOCK), BF16),
            pltpu.VMEM((2, 6, 2, 1, BLOCK), F32),
            pltpu.VMEM((2, 2, 1, BLOCK), F32),
            pltpu.VMEM((2, 2, 1, BLOCK), F32),
            pltpu.VMEM((2, 2, HEAD_DIM, BLOCK), F32),
            pltpu.VMEM((2, 2, HEAD_DIM, BLOCK), F32),
            pltpu.VMEM((2, 2, 1, BLOCK), F32),
            pltpu.VMEM((2, 2, 2, BLOCK, HEAD_DIM), F32),
            pltpu.VMEM(term, F32),
            pltpu.VMEM(term, BF16),
            pltpu.VMEM(term, BF16),
            pltpu.VMEM(term, BF16),
            pltpu.VMEM(term, BF16),
            pltpu.VMEM((4, 2, 2 * BLOCK, HEAD_DIM), BF16),
            dma((4, 2)), dma((4, 2)), dma((4, 2)),
            dma((2, 2, 2, 2, 2)), dma((2, 2, 2, 2, 2)),
            dma((2, 2, 2, 2)), dma((2, 2, 2, 2)), dma((2, 2, 2, 2)), dma((2, 2, 2, 2)),
            dma((4, 2)), dma((4, 2)), dma((4, 2)),
        ],
        compiler_params=pltpu.CompilerParams(
            collective_id=0, has_side_effects=True, vmem_limit_bytes=56 * 2 ** 20
        ),
        cost_estimate=pl.CostEstimate(
            flops=7 * 24 * 2 * BLOCK * BLOCK * HEAD_DIM, bytes_accessed=2 ** 22, transcendentals=24 * BLOCK * BLOCK
        ),
        name="butterfly_attention",
    )(queries, key_rows, value_rows, grad_out)


def solution(mesh):
    placed = P(("context", "ulysses"), None)
    return jax.shard_map(
        body, mesh=mesh, in_specs=(placed,) * 4, out_specs=(placed,) * 4, check_vma=False
    )
```

```python
import jax
import jax.numpy as jnp
from jax import lax
from jax.experimental import pallas as pl
from jax.experimental.pallas import tpu as pltpu
from jax.sharding import PartitionSpec as P

HEAD_DIM = 128
BLOCK = 512
ROWS = 128
F32 = jnp.float32
BF16 = jnp.bfloat16
SCALE = HEAD_DIM ** -0.5
EXP2_SCALE = SCALE * 1.4426950408889634
MESH = pl.DeviceIdType.MESH

KEY, VALUE, QUERY, GRAD = range(4)


def dot(a, b, ca, cb):
    return lax.dot_general(a, b, (((ca,), (cb,)), ((), ())), preferred_element_type=F32)


def kernel(
    q_in, k_in, v_in, g_in, out0, out1, out2, out3,
    kv, qg, qg_t, weights, peaks, run_peak, run_total, out_acc, query_acc, dots,
    acc, near, far_send, far_recv, near_send, near_recv, staged,
    in_send, in_recv, in_local, fwd_send, fwd_recv, far_ssem, far_rsem, near_ssem, near_rsem,
    out_send, out_recv, out_local,
):
    context = lax.axis_index("context")
    ulysses = lax.axis_index("ulysses")
    x = context // 8
    y = (context // 2) % 4
    z = (context % 2) * 2 + ulysses // 2
    core = ulysses % 2
    me = z * 2 + core

    def device(x, y, e):
        return {"context": x * 8 + y * 2 + e // 4, "ulysses": e % 4}

    def near_of(v):
        return v + 1 - 2 * (v % 2)

    def far_of(v):
        return 3 - v

    near_device = [device(near_of(x), y, me), device(x, near_of(y), me)]
    far_device = [device(far_of(x), y, me), device(x, far_of(y), me)]

    def remote(src, dst, ssem, rsem, to):
        return pltpu.make_async_remote_copy(
            src_ref=src, dst_ref=dst, send_sem=ssem, recv_sem=rsem, device_id=to, device_id_type=MESH
        )

    inputs = {KEY: k_in, VALUE: v_in, QUERY: q_in, GRAD: g_in}

    def landing(array, h):
        return kv.at[0, array, h] if array < 2 else qg.at[array - 2, h]

    def columns(e, h):
        return pl.ds(pl.multiple_of(e * 256 + h * 128, 128), 128)

    def rows_of(e):
        return pl.ds(pl.multiple_of(e * ROWS, ROWS), ROWS)

    order = [(KEY, 0), (VALUE, 0), (QUERY, 0), (KEY, 1), (VALUE, 1), (GRAD, 0), (QUERY, 1), (GRAD, 1)]

    def local_in(array, h):
        return pltpu.make_async_copy(
            inputs[array].at[:, columns(me, h)], landing(array, h).at[rows_of(me)], in_local.at[array, h]
        )

    for array, h in order:
        local_in(array, h).start()

    barrier = pltpu.get_barrier_semaphore()
    partners = [device(x, y, me ^ k) for k in range(1, 8)] + near_device + far_device
    for partner in partners:
        pl.semaphore_signal(barrier, inc=1, device_id=partner, device_id_type=MESH)
    pl.semaphore_wait(barrier, len(partners))

    def start_in(array, h, chip):
        for c in range(2):
            e = (z ^ chip) * 2 + (core ^ 1 if c == 0 else core)
            if chip or c == 0:
                remote(
                    inputs[array].at[:, columns(e, h)],
                    landing(array, h).at[rows_of(me)],
                    in_send.at[array, h],
                    in_recv.at[array, h, chip],
                    device(x, y, e),
                ).start()

    for array, h in order:
        if array < 2:
            start_in(array, h, 0)
    for array, h in order:
        for chip in (2, 3, 1):
            start_in(array, h, chip)
        if array >= 2:
            start_in(array, h, 0)

    def wait_in(array, h, chip):
        rows = ROWS if chip == 0 else 2 * ROWS
        part = landing(array, h).at[pl.ds(0, rows)]
        pltpu.make_async_copy(part, part, in_recv.at[array, h, chip]).wait()

    def wait_all_in(array, h):
        local_in(array, h).wait()
        for chip in range(4):
            wait_in(array, h, chip)

    z_hi = z // 2

    def at(i):
        return 1 - z_hi if i == 0 else z_hi

    def block_rows(s):
        return pl.ds(pl.multiple_of(s * BLOCK, BLOCK), BLOCK)

    def hop(axis, hop_at, array, h, chip):
        source = 0 if hop_at == 0 else 1 + 2 * axis
        rows = pl.ds(pl.multiple_of((z ^ chip) * 256, 256), 256)
        return remote(
            kv.at[source, array, h, rows],
            kv.at[1 + 2 * axis + hop_at, array, h, rows],
            fwd_send.at[axis, hop_at, array, h, chip],
            fwd_recv.at[axis, hop_at, array, h, chip],
            near_device[axis] if hop_at == 0 else far_device[axis],
        )

    CHIPS = (1, 3, 2)

    def start_own(array, h):
        local_in(array, h).wait()
        wait_in(array, h, 0)
        for axis in range(2):
            hop(axis, 0, array, h, 0).start()

    def start_near(array, h):
        for chip in CHIPS:
            wait_in(array, h, chip)
            for axis in range(2):
                hop(axis, 0, array, h, chip).start()

    def forward_far(array, h, chips=CHIPS):
        for chip in chips:
            for axis in range(2):
                hop(axis, 0, array, h, chip).wait_recv()
                hop(axis, 1, array, h, chip).start()

    def wait_far(array, h):
        for chip in (0,) + CHIPS:
            for axis in range(2):
                hop(axis, 1, array, h, chip).wait_recv()

    def turn(array, h):
        for s in range(2):
            qg_t[array - 2, h, s] = qg[array - 2, h, pl.ds(s * BLOCK, BLOCK), :].T

    def pair(j, h, s):
        source = 0 if j < 2 else j - 1
        rows = block_rows(1 - s if j == 1 else s)
        return kv[source, 0, h, rows, :], kv[source, 1, h, rows, :]

    def forward(j, h):
        def one(i, _):
            s = (1 - z_hi) ^ i
            keys, values = pair(j, h, s)
            scores = dot(keys, qg_t[0, h, s], 1, 0)
            peak = jnp.max(scores, axis=0, keepdims=True)
            shifted = jnp.exp2((scores - peak) * EXP2_SCALE)
            total = jnp.sum(shifted, axis=0, keepdims=True)
            low = shifted.astype(BF16)
            weights[h, j, s] = low
            peaks[h, j, s] = peak
            part = dot(values, low, 0, 0)
            if j == 0:
                run_peak[h, s] = peak
                run_total[h, s] = total
                out_acc[h, s] = part
            else:
                old = run_peak[h, s]
                joined = jnp.maximum(old, peak)
                keep = jnp.exp2((old - joined) * EXP2_SCALE)
                fresh = jnp.exp2((peak - joined) * EXP2_SCALE)
                run_peak[h, s] = joined
                run_total[h, s] = run_total[h, s] * keep + total * fresh
                out_acc[h, s] = out_acc[h, s] * keep + part * fresh
            return 0

        lax.fori_loop(0, 2, one, 0)

    outs = [out0, out1, out2, out3]

    def out_copy(array, h, e):
        return remote(
            staged.at[array, h, rows_of(e)],
            outs[array].at[:, columns(me, h)],
            out_send.at[array, h],
            out_recv.at[array, h],
            device(x, y, e),
        )

    def out_keep(array, h):
        return pltpu.make_async_copy(
            staged.at[array, h, rows_of(me)], outs[array].at[:, columns(me, h)], out_local.at[array, h]
        )

    def send_out(array, h, i):
        for chip in (2, 3) if i == 0 else (1, 0):
            for c in range(2):
                e = (z ^ chip) * 2 + (core ^ 1 if c == 0 else core)
                if chip or c == 0:
                    out_copy(array, h, e).start()
        if i == 1:
            out_keep(array, h).start()

    def finish_forward(h):
        for i in range(2):
            s = at(i)
            attended = (out_acc[h, s] / run_total[h, s]).astype(BF16)
            dots[h, s] = jnp.sum(attended.astype(F32) * qg_t[1, h, s].astype(F32), axis=0, keepdims=True)
            staged[0, h, block_rows(s)] = attended.T

    def finish_queries(h):
        for i in range(2):
            s = at(i)
            staged[1, h, block_rows(s)] = query_acc[h, s].astype(BF16).T
            send_out(1, h, i)

    def far_copy(axis, array, h, s):
        return remote(
            far_send.at[axis, array, h, s], far_recv.at[axis, array, h, s],
            far_ssem.at[axis, array, h, s], far_rsem.at[axis, array, h, s], far_device[axis],
        )

    def near_copy(axis, array, h, s):
        return remote(
            near_send.at[axis, array, h, s], near_recv.at[axis, array, h, s],
            near_ssem.at[axis, array, h, s], near_rsem.at[axis, array, h, s], near_device[axis],
        )

    def backward(j, h, first=False):
        axis = (j - 2) // 2

        def one(i, _):
            s = (1 - z_hi) ^ i
            keys, values = pair(j, h, s)
            low = weights[h, j, s]
            factor = jnp.exp2((peaks[h, j, s] - run_peak[h, s]) * EXP2_SCALE) / run_total[h, s]
            scaled = factor * SCALE
            grad_probs = dot(values, qg_t[1, h, s], 1, 0)
            grad_scores = (low.astype(F32) * (grad_probs - dots[h, s])).astype(BF16)
            query_part = dot(keys, grad_scores, 0, 0) * scaled
            if first:
                query_acc[h, s] = query_part
            else:
                query_acc[h, s] = query_acc[h, s] + query_part
            value_term = dot(low, (qg_t[1, h, s].astype(F32) * factor).astype(BF16), 1, 1)
            key_term = dot(grad_scores, (qg_t[0, h, s].astype(F32) * scaled).astype(BF16), 1, 1)
            if j == 0:
                acc[0, h, s] = key_term
                acc[1, h, s] = value_term
            elif j == 1:
                acc[0, h, 1 - s] = acc[0, h, 1 - s] + key_term
                acc[1, h, 1 - s] = acc[1, h, 1 - s] + value_term
            elif j % 2 == 0:
                near[axis, 0, h, s] = key_term
                near[axis, 1, h, s] = value_term
            else:
                far_send[axis, 0, h, s] = key_term.astype(BF16)
                far_send[axis, 1, h, s] = value_term.astype(BF16)
            return 0

        lax.fori_loop(0, 2, one, 0)

    def send_far(axis, h):
        for i in range(2):
            for array in range(2):
                far_copy(axis, array, h, at(i)).start()

    def reduce_near(h, i, array):
        s = at(i)
        for axis in range(2):
            far_copy(axis, array, h, s).wait_recv()
            near_send[axis, array, h, s] = (
                near[axis, array, h, s] + far_recv[axis, array, h, s].astype(F32)
            ).astype(BF16)
            near_copy(axis, array, h, s).start()

    def finish_keys(h, i, array):
        s = at(i)
        total = acc[array, h, s]
        for axis in range(2):
            near_copy(axis, array, h, s).wait_recv()
            total = total + near_recv[axis, array, h, s].astype(F32)
        staged[2 + array, h, block_rows(s)] = total.astype(BF16)
        send_out(2 + array, h, i)

    for array, h in order:
        if array < 2:
            start_own(array, h)
    start_near(KEY, 0)
    forward_far(KEY, 0, (0,))
    forward_far(VALUE, 0, (0,))
    start_near(VALUE, 0)
    forward_far(KEY, 1, (0,))
    forward_far(VALUE, 1, (0,))
    wait_all_in(QUERY, 0)
    turn(QUERY, 0)
    forward(0, 0)
    forward_far(KEY, 0)
    start_near(KEY, 1)
    forward(1, 0)
    forward_far(VALUE, 0)
    start_near(VALUE, 1)
    forward(2, 0)
    forward(4, 0)
    forward_far(KEY, 1)
    wait_all_in(GRAD, 0)
    turn(GRAD, 0)
    wait_far(KEY, 0)
    wait_far(VALUE, 0)
    forward(3, 0)
    forward(5, 0)
    finish_forward(0)
    forward_far(VALUE, 1)
    backward(3, 0, first=True)
    send_far(0, 0)
    backward(5, 0)
    send_far(1, 0)
    send_out(0, 0, 0)
    send_out(0, 0, 1)
    backward(2, 0)
    backward(4, 0)
    wait_all_in(QUERY, 1)
    turn(QUERY, 1)
    forward(0, 1)
    reduce_near(0, 0, 0)
    forward(1, 1)
    reduce_near(0, 0, 1)
    forward(2, 1)
    wait_all_in(GRAD, 1)
    turn(GRAD, 1)
    forward(4, 1)
    wait_far(KEY, 1)
    wait_far(VALUE, 1)
    forward(3, 1)
    forward(5, 1)
    finish_forward(1)
    backward(3, 1, first=True)
    send_far(0, 1)
    reduce_near(0, 1, 0)
    backward(5, 1)
    send_far(1, 1)
    reduce_near(0, 1, 1)
    send_out(0, 1, 0)
    send_out(0, 1, 1)
    backward(2, 1)
    backward(4, 1)
    reduce_near(1, 0, 0)
    backward(0, 0)
    reduce_near(1, 0, 1)
    backward(1, 0)
    finish_queries(0)
    backward(0, 1)
    reduce_near(1, 1, 0)
    backward(1, 1)
    finish_queries(1)
    finish_keys(0, 0, 0)
    finish_keys(0, 0, 1)
    reduce_near(1, 1, 1)
    finish_keys(0, 1, 0)
    finish_keys(0, 1, 1)
    finish_keys(1, 0, 0)
    finish_keys(1, 0, 1)
    finish_keys(1, 1, 0)
    finish_keys(1, 1, 1)

    for array in range(4):
        for h in range(2):
            part = landing(array, h).at[pl.ds(0, 7 * ROWS)]
            pltpu.make_async_copy(part, part, in_send.at[array, h]).wait()
    for array in range(2):
        for h in range(2):
            for axis in range(2):
                for chip in range(4):
                    hop(axis, 0, array, h, chip).wait_send()
                    hop(axis, 1, array, h, chip).wait_send()
                for s in range(2):
                    far_copy(axis, array, h, s).wait_send()
                    near_copy(axis, array, h, s).wait_send()
    for array in range(4):
        for h in range(2):
            out_keep(array, h).wait()
            part = staged.at[array, h, pl.ds(0, 7 * ROWS)]
            pltpu.make_async_copy(part, part, out_send.at[array, h]).wait()
            pltpu.make_async_copy(part, part, out_recv.at[array, h]).wait()


def body(queries, key_rows, value_rows, grad_out):
    dma = pltpu.SemaphoreType.DMA
    term = (2, 2, 2, 2, BLOCK, HEAD_DIM)
    shape = jax.ShapeDtypeStruct(queries.shape, BF16)
    return pl.pallas_call(
        kernel,
        out_shape=[shape] * 4,
        in_specs=[pl.BlockSpec(memory_space=pl.ANY)] * 4,
        out_specs=[pl.BlockSpec(memory_space=pl.ANY)] * 4,
        scratch_shapes=[
            pltpu.VMEM((5, 2, 2, 2 * BLOCK, HEAD_DIM), BF16),
            pltpu.VMEM((2, 2, 2 * BLOCK, HEAD_DIM), BF16),
            pltpu.VMEM((2, 2, 2, HEAD_DIM, BLOCK), BF16),
            pltpu.VMEM((2, 6, 2, BLOCK, BLOCK), BF16),
            pltpu.VMEM((2, 6, 2, 1, BLOCK), F32),
            pltpu.VMEM((2, 2, 1, BLOCK), F32),
            pltpu.VMEM((2, 2, 1, BLOCK), F32),
            pltpu.VMEM((2, 2, HEAD_DIM, BLOCK), F32),
            pltpu.VMEM((2, 2, HEAD_DIM, BLOCK), F32),
            pltpu.VMEM((2, 2, 1, BLOCK), F32),
            pltpu.VMEM((2, 2, 2, BLOCK, HEAD_DIM), F32),
            pltpu.VMEM(term, F32),
            pltpu.VMEM(term, BF16),
            pltpu.VMEM(term, BF16),
            pltpu.VMEM(term, BF16),
            pltpu.VMEM(term, BF16),
            pltpu.VMEM((4, 2, 2 * BLOCK, HEAD_DIM), BF16),
            dma((4, 2)), dma((4, 2, 4)), dma((4, 2)),
            dma((2, 2, 2, 2, 4)), dma((2, 2, 2, 2, 4)),
            dma((2, 2, 2, 2)), dma((2, 2, 2, 2)), dma((2, 2, 2, 2)), dma((2, 2, 2, 2)),
            dma((4, 2)), dma((4, 2)), dma((4, 2)),
        ],
        compiler_params=pltpu.CompilerParams(
            collective_id=0, has_side_effects=True, vmem_limit_bytes=103 * 2 ** 19
        ),
        cost_estimate=pl.CostEstimate(
            flops=7 * 24 * 2 * BLOCK * BLOCK * HEAD_DIM, bytes_accessed=2 ** 22, transcendentals=24 * BLOCK * BLOCK
        ),
        name="butterfly_attention",
    )(queries, key_rows, value_rows, grad_out)


def solution(mesh):
    placed = P(("context", "ulysses"), None)
    return jax.shard_map(
        body, mesh=mesh, in_specs=(placed,) * 4, out_specs=(placed,) * 4, check_vma=False
    )
```

```python
import jax
import jax.numpy as jnp
from jax import lax
from jax.experimental import pallas as pl
from jax.experimental.pallas import tpu as pltpu
from jax.sharding import PartitionSpec as P

HEAD_DIM = 128
BLOCK = 512
ROWS = 128
F32 = jnp.float32
BF16 = jnp.bfloat16
SCALE = HEAD_DIM ** -0.5
EXP2_SCALE = SCALE * 1.4426950408889634
MESH = pl.DeviceIdType.MESH

KEY, VALUE, QUERY, GRAD = range(4)


def dot(a, b, ca, cb):
    return lax.dot_general(a, b, (((ca,), (cb,)), ((), ())), preferred_element_type=F32)


def kernel(
    q_in, k_in, v_in, g_in, out0, out1, out2, out3,
    kv, qg, qg_t, weights, peaks, run_peak, run_total, out_acc, query_acc, dots,
    acc, near, far_send, far_recv, near_send, near_recv, staged,
    in_send, in_recv, in_local, fwd_send, fwd_recv, far_ssem, far_rsem, near_ssem, near_rsem,
    out_send, out_recv, out_local,
):
    context = lax.axis_index("context")
    ulysses = lax.axis_index("ulysses")
    x = context // 8
    y = (context // 2) % 4
    z = (context % 2) * 2 + ulysses // 2
    core = ulysses % 2
    me = z * 2 + core

    def device(x, y, e):
        return {"context": x * 8 + y * 2 + e // 4, "ulysses": e % 4}

    def near_of(v):
        return v + 1 - 2 * (v % 2)

    def far_of(v):
        return 3 - v

    near_device = [device(near_of(x), y, me), device(x, near_of(y), me)]
    far_device = [device(far_of(x), y, me), device(x, far_of(y), me)]

    def remote(src, dst, ssem, rsem, to):
        return pltpu.make_async_remote_copy(
            src_ref=src, dst_ref=dst, send_sem=ssem, recv_sem=rsem, device_id=to, device_id_type=MESH
        )

    inputs = {KEY: k_in, VALUE: v_in, QUERY: q_in, GRAD: g_in}

    def landing(array, h):
        return kv.at[0, array, h] if array < 2 else qg.at[array - 2, h]

    def columns(e, h):
        return pl.ds(pl.multiple_of(e * 256 + h * 128, 128), 128)

    def rows_of(e):
        return pl.ds(pl.multiple_of(e * ROWS, ROWS), ROWS)

    order = [(KEY, 0), (VALUE, 0), (QUERY, 0), (KEY, 1), (VALUE, 1), (GRAD, 0), (QUERY, 1), (GRAD, 1)]

    def local_in(array, h):
        return pltpu.make_async_copy(
            inputs[array].at[:, columns(me, h)], landing(array, h).at[rows_of(me)], in_local.at[array, h]
        )

    for array, h in order:
        local_in(array, h).start()

    barrier = pltpu.get_barrier_semaphore()
    partners = [device(x, y, me ^ k) for k in range(1, 8)] + near_device + far_device
    for partner in partners:
        pl.semaphore_signal(barrier, inc=1, device_id=partner, device_id_type=MESH)
    pl.semaphore_wait(barrier, len(partners))

    def start_in(array, h, chip):
        for c in range(2):
            e = (z ^ chip) * 2 + (core ^ 1 if c == 0 else core)
            if chip or c == 0:
                remote(
                    inputs[array].at[:, columns(e, h)],
                    landing(array, h).at[rows_of(me)],
                    in_send.at[array, h],
                    in_recv.at[array, h, chip],
                    device(x, y, e),
                ).start()

    for array, h in order:
        if array < 2:
            start_in(array, h, 0)
    for array, h in order:
        for chip in (2, 3, 1):
            start_in(array, h, chip)
        if array >= 2:
            start_in(array, h, 0)

    def wait_in(array, h, chip):
        rows = ROWS if chip == 0 else 2 * ROWS
        part = landing(array, h).at[pl.ds(0, rows)]
        pltpu.make_async_copy(part, part, in_recv.at[array, h, chip]).wait()

    def wait_all_in(array, h):
        local_in(array, h).wait()
        for chip in range(4):
            wait_in(array, h, chip)

    z_hi = z // 2

    def at(i):
        return 1 - z_hi if i == 0 else z_hi

    def block_rows(s):
        return pl.ds(pl.multiple_of(s * BLOCK, BLOCK), BLOCK)

    def hop(axis, hop_at, array, h, chip):
        source = 0 if hop_at == 0 else 1 + 2 * axis
        rows = pl.ds(pl.multiple_of((z ^ chip) * 256, 256), 256)
        return remote(
            kv.at[source, array, h, rows],
            kv.at[1 + 2 * axis + hop_at, array, h, rows],
            fwd_send.at[axis, hop_at, array, h, chip],
            fwd_recv.at[axis, hop_at, array, h, chip],
            near_device[axis] if hop_at == 0 else far_device[axis],
        )

    CHIPS = (1, 3, 2)

    def start_own(array, h):
        local_in(array, h).wait()
        wait_in(array, h, 0)
        for axis in range(2):
            hop(axis, 0, array, h, 0).start()

    def start_near(array, h):
        for chip in CHIPS:
            wait_in(array, h, chip)
            for axis in range(2):
                hop(axis, 0, array, h, chip).start()

    def forward_far(array, h, chips=CHIPS):
        for chip in chips:
            for axis in range(2):
                hop(axis, 0, array, h, chip).wait_recv()
                hop(axis, 1, array, h, chip).start()

    def wait_far(array, h):
        for chip in (0,) + CHIPS:
            for axis in range(2):
                hop(axis, 1, array, h, chip).wait_recv()

    def turn(array, h):
        for s in range(2):
            qg_t[array - 2, h, s] = qg[array - 2, h, pl.ds(s * BLOCK, BLOCK), :].T

    def pair(j, h, s):
        source = 0 if j < 2 else j - 1
        rows = block_rows(1 - s if j == 1 else s)
        return kv[source, 0, h, rows, :], kv[source, 1, h, rows, :]

    def forward(j, h):
        def one(i, _):
            s = (1 - z_hi) ^ i
            keys, values = pair(j, h, s)
            scores = dot(keys, qg_t[0, h, s], 1, 0)
            peak = jnp.max(scores, axis=0, keepdims=True)
            shifted = jnp.exp2((scores - peak) * EXP2_SCALE)
            total = jnp.sum(shifted, axis=0, keepdims=True)
            low = shifted.astype(BF16)
            weights[h, j, s] = low
            peaks[h, j, s] = peak
            part = dot(values, low, 0, 0)
            if j == 0:
                run_peak[h, s] = peak
                run_total[h, s] = total
                out_acc[h, s] = part
            else:
                old = run_peak[h, s]
                joined = jnp.maximum(old, peak)
                keep = jnp.exp2((old - joined) * EXP2_SCALE)
                fresh = jnp.exp2((peak - joined) * EXP2_SCALE)
                run_peak[h, s] = joined
                run_total[h, s] = run_total[h, s] * keep + total * fresh
                out_acc[h, s] = out_acc[h, s] * keep + part * fresh
            return 0

        for i in range(2):
            one(i, 0)

    outs = [out0, out1, out2, out3]

    def out_copy(array, h, e):
        return remote(
            staged.at[array, h, rows_of(e)],
            outs[array].at[:, columns(me, h)],
            out_send.at[array, h],
            out_recv.at[array, h],
            device(x, y, e),
        )

    def out_keep(array, h):
        return pltpu.make_async_copy(
            staged.at[array, h, rows_of(me)], outs[array].at[:, columns(me, h)], out_local.at[array, h]
        )

    def send_out(array, h, i):
        for chip in (2, 3) if i == 0 else (1, 0):
            for c in range(2):
                e = (z ^ chip) * 2 + (core ^ 1 if c == 0 else core)
                if chip or c == 0:
                    out_copy(array, h, e).start()
        if i == 1:
            out_keep(array, h).start()

    def finish_forward(h):
        for i in range(2):
            s = at(i)
            attended = (out_acc[h, s] / run_total[h, s]).astype(BF16)
            dots[h, s] = jnp.sum(attended.astype(F32) * qg_t[1, h, s].astype(F32), axis=0, keepdims=True)
            staged[0, h, block_rows(s)] = attended.T

    def finish_queries(h):
        for i in range(2):
            s = at(i)
            staged[1, h, block_rows(s)] = query_acc[h, s].astype(BF16).T
            send_out(1, h, i)

    def far_copy(axis, array, h, s):
        return remote(
            far_send.at[axis, array, h, s], far_recv.at[axis, array, h, s],
            far_ssem.at[axis, array, h, s], far_rsem.at[axis, array, h, s], far_device[axis],
        )

    def near_copy(axis, array, h, s):
        return remote(
            near_send.at[axis, array, h, s], near_recv.at[axis, array, h, s],
            near_ssem.at[axis, array, h, s], near_rsem.at[axis, array, h, s], near_device[axis],
        )

    def backward(j, h, first=False):
        axis = (j - 2) // 2

        def one(i, _):
            s = (1 - z_hi) ^ i
            keys, values = pair(j, h, s)
            low = weights[h, j, s]
            factor = jnp.exp2((peaks[h, j, s] - run_peak[h, s]) * EXP2_SCALE) / run_total[h, s]
            scaled = factor * SCALE
            grad_probs = dot(values, qg_t[1, h, s], 1, 0)
            grad_scores = (low.astype(F32) * (grad_probs - dots[h, s])).astype(BF16)
            query_part = dot(keys, grad_scores, 0, 0) * scaled
            if first:
                query_acc[h, s] = query_part
            else:
                query_acc[h, s] = query_acc[h, s] + query_part
            value_term = dot(low, (qg_t[1, h, s].astype(F32) * factor).astype(BF16), 1, 1)
            key_term = dot(grad_scores, (qg_t[0, h, s].astype(F32) * scaled).astype(BF16), 1, 1)
            if j == 0:
                acc[0, h, s] = key_term
                acc[1, h, s] = value_term
            elif j == 1:
                acc[0, h, 1 - s] = acc[0, h, 1 - s] + key_term
                acc[1, h, 1 - s] = acc[1, h, 1 - s] + value_term
            elif j % 2 == 0:
                near[axis, 0, h, s] = key_term
                near[axis, 1, h, s] = value_term
            else:
                far_send[axis, 0, h, s] = key_term.astype(BF16)
                far_send[axis, 1, h, s] = value_term.astype(BF16)
            return 0

        for i in range(2):
            one(i, 0)

    def send_far(axis, h):
        for i in range(2):
            for array in range(2):
                far_copy(axis, array, h, at(i)).start()

    def reduce_near(h, i, array):
        s = at(i)
        for axis in range(2):
            far_copy(axis, array, h, s).wait_recv()
            near_send[axis, array, h, s] = (
                near[axis, array, h, s] + far_recv[axis, array, h, s].astype(F32)
            ).astype(BF16)
            near_copy(axis, array, h, s).start()

    def finish_keys(h, i, array):
        s = at(i)
        total = acc[array, h, s]
        for axis in range(2):
            near_copy(axis, array, h, s).wait_recv()
            total = total + near_recv[axis, array, h, s].astype(F32)
        staged[2 + array, h, block_rows(s)] = total.astype(BF16)
        send_out(2 + array, h, i)

    for array, h in order:
        if array < 2:
            start_own(array, h)
    start_near(KEY, 0)
    forward_far(KEY, 0, (0,))
    forward_far(VALUE, 0, (0,))
    start_near(VALUE, 0)
    forward_far(KEY, 1, (0,))
    forward_far(VALUE, 1, (0,))
    wait_all_in(QUERY, 0)
    turn(QUERY, 0)
    forward(0, 0)
    forward_far(KEY, 0)
    start_near(KEY, 1)
    forward(1, 0)
    forward_far(VALUE, 0)
    start_near(VALUE, 1)
    forward(2, 0)
    forward(4, 0)
    forward_far(KEY, 1)
    wait_all_in(GRAD, 0)
    turn(GRAD, 0)
    wait_far(KEY, 0)
    wait_far(VALUE, 0)
    forward(3, 0)
    forward(5, 0)
    finish_forward(0)
    backward(3, 0, first=True)
    backward(5, 0)
    backward(2, 0)
    forward_far(VALUE, 1)
    send_far(0, 0)
    send_far(1, 0)
    send_out(0, 0, 0)
    send_out(0, 0, 1)
    backward(4, 0)
    wait_all_in(QUERY, 1)
    turn(QUERY, 1)
    backward(0, 0)
    backward(1, 0)
    finish_queries(0)
    forward(0, 1)
    reduce_near(0, 0, 0)
    forward(1, 1)
    wait_all_in(GRAD, 1)
    turn(GRAD, 1)
    forward(2, 1)
    reduce_near(0, 0, 1)
    forward(4, 1)
    wait_far(KEY, 1)
    wait_far(VALUE, 1)
    forward(3, 1)
    reduce_near(0, 1, 0)
    forward(5, 1)
    finish_forward(1)
    backward(3, 1, first=True)
    send_far(0, 1)
    backward(5, 1)
    send_far(1, 1)
    reduce_near(0, 1, 1)
    send_out(0, 1, 0)
    send_out(0, 1, 1)
    backward(2, 1)
    finish_keys(0, 0, 0)
    backward(4, 1)
    finish_keys(0, 0, 1)
    reduce_near(1, 0, 0)
    backward(0, 1)
    finish_keys(0, 1, 0)
    backward(1, 1)
    finish_queries(1)
    reduce_near(1, 0, 1)
    finish_keys(0, 1, 1)
    reduce_near(1, 1, 0)
    finish_keys(1, 0, 0)
    reduce_near(1, 1, 1)
    finish_keys(1, 0, 1)
    finish_keys(1, 1, 0)
    finish_keys(1, 1, 1)

    for array in range(4):
        for h in range(2):
            part = landing(array, h).at[pl.ds(0, 7 * ROWS)]
            pltpu.make_async_copy(part, part, in_send.at[array, h]).wait()
    for array in range(2):
        for h in range(2):
            for axis in range(2):
                for chip in range(4):
                    hop(axis, 0, array, h, chip).wait_send()
                    hop(axis, 1, array, h, chip).wait_send()
                for s in range(2):
                    far_copy(axis, array, h, s).wait_send()
                    near_copy(axis, array, h, s).wait_send()
    for array in range(4):
        for h in range(2):
            out_keep(array, h).wait()
            part = staged.at[array, h, pl.ds(0, 7 * ROWS)]
            pltpu.make_async_copy(part, part, out_send.at[array, h]).wait()
            pltpu.make_async_copy(part, part, out_recv.at[array, h]).wait()


def keep_kernel(in0, in1, in2, in3, out0, out1, out2, out3, done):
    copies = [
        pltpu.make_async_copy(src, dst, done.at[i])
        for i, (src, dst) in enumerate(((in0, out0), (in1, out1), (in2, out2), (in3, out3)))
    ]
    for copy in copies:
        copy.start()
    for copy in copies:
        copy.wait()


def body(queries, key_rows, value_rows, grad_out):
    dma = pltpu.SemaphoreType.DMA
    term = (2, 2, 2, 2, BLOCK, HEAD_DIM)
    shape = jax.ShapeDtypeStruct(queries.shape, BF16)
    results = pl.pallas_call(
        kernel,
        out_shape=[shape] * 4,
        in_specs=[pl.BlockSpec(memory_space=pl.ANY)] * 4,
        out_specs=[pl.BlockSpec(memory_space=pl.ANY)] * 4,
        scratch_shapes=[
            pltpu.VMEM((5, 2, 2, 2 * BLOCK, HEAD_DIM), BF16),
            pltpu.VMEM((2, 2, 2 * BLOCK, HEAD_DIM), BF16),
            pltpu.VMEM((2, 2, 2, HEAD_DIM, BLOCK), BF16),
            pltpu.VMEM((2, 6, 2, BLOCK, BLOCK), BF16),
            pltpu.VMEM((2, 6, 2, 1, BLOCK), F32),
            pltpu.VMEM((2, 2, 1, BLOCK), F32),
            pltpu.VMEM((2, 2, 1, BLOCK), F32),
            pltpu.VMEM((2, 2, HEAD_DIM, BLOCK), F32),
            pltpu.VMEM((2, 2, HEAD_DIM, BLOCK), F32),
            pltpu.VMEM((2, 2, 1, BLOCK), F32),
            pltpu.VMEM((2, 2, 2, BLOCK, HEAD_DIM), F32),
            pltpu.VMEM(term, F32),
            pltpu.VMEM(term, BF16),
            pltpu.VMEM(term, BF16),
            pltpu.VMEM(term, BF16),
            pltpu.VMEM(term, BF16),
            pltpu.VMEM((4, 2, 2 * BLOCK, HEAD_DIM), BF16),
            dma((4, 2)), dma((4, 2, 4)), dma((4, 2)),
            dma((2, 2, 2, 2, 4)), dma((2, 2, 2, 2, 4)),
            dma((2, 2, 2, 2)), dma((2, 2, 2, 2)), dma((2, 2, 2, 2)), dma((2, 2, 2, 2)),
            dma((4, 2)), dma((4, 2)), dma((4, 2)),
        ],
        compiler_params=pltpu.CompilerParams(
            collective_id=0, has_side_effects=True, vmem_limit_bytes=103 * 2 ** 19
        ),
        cost_estimate=pl.CostEstimate(
            flops=7 * 24 * 2 * BLOCK * BLOCK * HEAD_DIM, bytes_accessed=2 ** 22, transcendentals=24 * BLOCK * BLOCK
        ),
        name="butterfly_attention",
    )(queries, key_rows, value_rows, grad_out)
    return pl.pallas_call(
        keep_kernel,
        out_shape=[shape] * 4,
        in_specs=[pl.BlockSpec(memory_space=pl.ANY)] * 4,
        out_specs=[pl.BlockSpec(memory_space=pl.ANY)] * 4,
        scratch_shapes=[dma((4,))],
        name="keep_results",
    )(*results)


def solution(mesh):
    placed = P(("context", "ulysses"), None)
    return jax.shard_map(
        body, mesh=mesh, in_specs=(placed,) * 4, out_specs=(placed,) * 4, check_vma=False
    )
```

```python
import jax
import jax.numpy as jnp
from jax import lax
from jax.experimental import pallas as pl
from jax.experimental.pallas import tpu as pltpu
from jax.sharding import PartitionSpec as P

HEAD_DIM = 128
BLOCK = 512
ROWS = 128
F32 = jnp.float32
BF16 = jnp.bfloat16
SCALE = HEAD_DIM ** -0.5
EXP2_SCALE = SCALE * 1.4426950408889634
MESH = pl.DeviceIdType.MESH

KEY, VALUE, QUERY, GRAD = range(4)
GROUPS = ((0, 1), (2, 4), (3, 5))


def dot(a, b, ca, cb):
    return lax.dot_general(a, b, (((ca,), (cb,)), ((), ())), preferred_element_type=F32)


def kernel(
    q_in, k_in, v_in, g_in, out0, out1, out2, out3,
    kv, qg, qg_t, weights, peaks, run_peak, run_total, out_acc, query_acc, dots,
    acc, near, far_send, far_recv, near_send, near_recv, staged,
    in_send, in_recv, in_local, fwd_send, fwd_recv, far_ssem, far_rsem, near_ssem, near_rsem,
    out_send, out_recv, out_local,
):
    context = lax.axis_index("context")
    ulysses = lax.axis_index("ulysses")
    x = context // 8
    y = (context // 2) % 4
    z = (context % 2) * 2 + ulysses // 2
    core = ulysses % 2
    me = z * 2 + core

    def device(x, y, e):
        return {"context": x * 8 + y * 2 + e // 4, "ulysses": e % 4}

    def near_of(v):
        return v + 1 - 2 * (v % 2)

    def far_of(v):
        return 3 - v

    near_device = [device(near_of(x), y, me), device(x, near_of(y), me)]
    far_device = [device(far_of(x), y, me), device(x, far_of(y), me)]

    def remote(src, dst, ssem, rsem, to):
        return pltpu.make_async_remote_copy(
            src_ref=src, dst_ref=dst, send_sem=ssem, recv_sem=rsem, device_id=to, device_id_type=MESH
        )

    inputs = {KEY: k_in, VALUE: v_in, QUERY: q_in, GRAD: g_in}

    def landing(array, h):
        return kv.at[0, array, h] if array < 2 else qg.at[array - 2, h]

    def columns(e, h):
        return pl.ds(pl.multiple_of(e * 256 + h * 128, 128), 128)

    def rows_of(e):
        return pl.ds(pl.multiple_of(e * ROWS, ROWS), ROWS)

    order = [(KEY, 0), (VALUE, 0), (QUERY, 0), (KEY, 1), (VALUE, 1), (GRAD, 0), (QUERY, 1), (GRAD, 1)]

    def local_in(array, h):
        return pltpu.make_async_copy(
            inputs[array].at[:, columns(me, h)], landing(array, h).at[rows_of(me)], in_local.at[array, h]
        )

    for array, h in order:
        local_in(array, h).start()

    barrier = pltpu.get_barrier_semaphore()
    partners = [device(x, y, me ^ k) for k in range(1, 8)] + near_device + far_device
    for partner in partners:
        pl.semaphore_signal(barrier, inc=1, device_id=partner, device_id_type=MESH)
    pl.semaphore_wait(barrier, len(partners))

    def start_in(array, h, chip):
        for c in range(2):
            e = (z ^ chip) * 2 + (core ^ 1 if c == 0 else core)
            if chip or c == 0:
                remote(
                    inputs[array].at[:, columns(e, h)],
                    landing(array, h).at[rows_of(me)],
                    in_send.at[array, h],
                    in_recv.at[array, h, chip],
                    device(x, y, e),
                ).start()

    def wait_in(array, h, chip):
        rows = ROWS if chip == 0 else 2 * ROWS
        part = landing(array, h).at[pl.ds(0, rows)]
        pltpu.make_async_copy(part, part, in_recv.at[array, h, chip]).wait()

    def wait_all_in(array, h):
        local_in(array, h).wait()
        for chip in range(4):
            wait_in(array, h, chip)

    z_hi = z // 2

    def at(i):
        return 1 - z_hi if i == 0 else z_hi

    def block_rows(s):
        return pl.ds(pl.multiple_of(s * BLOCK, BLOCK), BLOCK)

    def hop(axis, hop_at, array, h, chip):
        source = 0 if hop_at == 0 else 1 + 2 * axis
        rows = pl.ds(pl.multiple_of((z ^ chip) * 256, 256), 256)
        return remote(
            kv.at[source, array, h, rows],
            kv.at[1 + 2 * axis + hop_at, array, h, rows],
            fwd_send.at[axis, hop_at, array, h, chip],
            fwd_recv.at[axis, hop_at, array, h, chip],
            near_device[axis] if hop_at == 0 else far_device[axis],
        )

    CHIPS = (1, 3, 2)

    def start_own(array, h, e):
        for axis in range(2):
            remote(
                kv.at[0, array, h, rows_of(e)],
                kv.at[1 + 2 * axis, array, h, rows_of(e)],
                fwd_send.at[axis, 0, array, h, 0],
                fwd_recv.at[axis, 0, array, h, 0],
                near_device[axis],
            ).start()

    def start_near(array, h):
        for chip in CHIPS:
            wait_in(array, h, chip)
            for axis in range(2):
                hop(axis, 0, array, h, chip).start()

    def pass_on(array, h, chip):
        for axis in range(2):
            hop(axis, 0, array, h, chip).wait_recv()
            hop(axis, 1, array, h, chip).start()

    def wait_far(h, chips):
        for chip in chips:
            for array in range(2):
                for axis in range(2):
                    hop(axis, 1, array, h, chip).wait_recv()

    def turn(array, h):
        for s in range(2):
            qg_t[array - 2, h, s] = qg[array - 2, h, pl.ds(s * BLOCK, BLOCK), :].T

    def pair(j, h, s):
        source = 0 if j < 2 else j - 1
        rows = block_rows(1 - s if j == 1 else s)
        return kv[source, 0, h, rows, :], kv[source, 1, h, rows, :]

    def forward(group, h, i):
        s = at(i)
        pairs = [pair(j, h, s) for j in GROUPS[group]]
        scores = [dot(keys, qg_t[0, h, s], 1, 0) for keys, _ in pairs]
        peak = jnp.maximum(*[jnp.max(each, axis=0, keepdims=True) for each in scores])
        total, part = 0.0, 0.0
        for j, each, (_, values) in zip(GROUPS[group], scores, pairs):
            shifted = jnp.exp2((each - peak) * EXP2_SCALE)
            total = total + jnp.sum(shifted, axis=0, keepdims=True)
            low = shifted.astype(BF16)
            weights[h, j, s] = low
            part = part + dot(values, low, 0, 0)
        peaks[h, group, s] = peak
        if group == 0:
            run_peak[h, s] = peak
            run_total[h, s] = total
            out_acc[h, s] = part
        else:
            old = run_peak[h, s]
            joined = jnp.maximum(old, peak)
            keep = jnp.exp2((old - joined) * EXP2_SCALE)
            fresh = jnp.exp2((peak - joined) * EXP2_SCALE)
            run_peak[h, s] = joined
            run_total[h, s] = run_total[h, s] * keep + total * fresh
            out_acc[h, s] = out_acc[h, s] * keep + part * fresh

    outs = [out0, out1, out2, out3]

    def out_copy(array, h, e):
        return remote(
            staged.at[array, h, rows_of(e)],
            outs[array].at[:, columns(me, h)],
            out_send.at[array, h],
            out_recv.at[array, h],
            device(x, y, e),
        )

    def out_keep(array, h):
        return pltpu.make_async_copy(
            staged.at[array, h, rows_of(me)], outs[array].at[:, columns(me, h)], out_local.at[array, h]
        )

    def send_out(array, h, i):
        for chip in (2, 3) if i == 0 else (1, 0):
            for c in range(2):
                e = (z ^ chip) * 2 + (core ^ 1 if c == 0 else core)
                if chip or c == 0:
                    out_copy(array, h, e).start()
        if i == 1:
            out_keep(array, h).start()

    def finish_forward(h):
        for i in range(2):
            s = at(i)
            attended = (out_acc[h, s] / run_total[h, s]).astype(BF16)
            dots[h, s] = jnp.sum(attended.astype(F32) * qg_t[1, h, s].astype(F32), axis=0, keepdims=True)
            staged[0, h, block_rows(s)] = attended.T

    def finish_queries(h):
        for i in range(2):
            s = at(i)
            staged[1, h, block_rows(s)] = query_acc[h, s].astype(BF16).T
            send_out(1, h, i)

    def far_copy(axis, array, h, s):
        return remote(
            far_send.at[axis, array, h, s], far_recv.at[axis, array, h, s],
            far_ssem.at[axis, array, h, s], far_rsem.at[axis, array, h, s], far_device[axis],
        )

    def near_copy(axis, array, h, s):
        return remote(
            near_send.at[axis, array, h, s], near_recv.at[axis, array, h, s],
            near_ssem.at[axis, array, h, s], near_rsem.at[axis, array, h, s], near_device[axis],
        )

    def backward(group, h, i):
        s = at(i)
        factor = jnp.exp2((peaks[h, group, s] - run_peak[h, s]) * EXP2_SCALE) / run_total[h, s]
        scaled = factor * SCALE
        grads = qg_t[1, h, s]
        grads_scaled = (grads.astype(F32) * factor).astype(BF16)
        queries_scaled = (qg_t[0, h, s].astype(F32) * scaled).astype(BF16)
        query_part = 0.0
        for j in GROUPS[group]:
            axis = (j - 2) // 2
            keys, values = pair(j, h, s)
            low = weights[h, j, s]
            grad_probs = dot(values, grads, 1, 0)
            grad_scores = (low.astype(F32) * (grad_probs - dots[h, s])).astype(BF16)
            query_part = query_part + dot(keys, grad_scores, 0, 0)
            value_term = dot(low, grads_scaled, 1, 1)
            key_term = dot(grad_scores, queries_scaled, 1, 1)
            for array, term in ((0, key_term), (1, value_term)):
                if group == 2:
                    far_send[axis, array, h, s] = term.astype(BF16)
                elif group == 1:
                    near[axis, array, h, s] = term
                elif i == 0:
                    acc[array, h, s if j == 0 else 1 - s] = term
                else:
                    place = s if j == 0 else 1 - s
                    acc[array, h, place] = acc[array, h, place] + term
        if group == 2:
            query_acc[h, s] = query_part * scaled
        else:
            query_acc[h, s] = query_acc[h, s] + query_part * scaled

    def send_far(h, i):
        for array in range(2):
            for axis in range(2):
                far_copy(axis, array, h, at(i)).start()

    def reduce_near(h, i, array):
        s = at(i)
        for axis in range(2):
            far_copy(axis, array, h, s).wait_recv()
            near_send[axis, array, h, s] = (
                near[axis, array, h, s] + far_recv[axis, array, h, s].astype(F32)
            ).astype(BF16)
            near_copy(axis, array, h, s).start()

    def finish_keys(h, i, array):
        s = at(i)
        total = acc[array, h, s]
        for axis in range(2):
            near_copy(axis, array, h, s).wait_recv()
            total = total + near_recv[axis, array, h, s].astype(F32)
        staged[2 + array, h, block_rows(s)] = total.astype(BF16)
        send_out(2 + array, h, i)

    def start_all_in(array, h):
        for chip in (2, 3, 1) if array < 2 else (2, 3, 1, 0):
            start_in(array, h, chip)

    first = ((KEY, 0), (VALUE, 0), (KEY, 1), (VALUE, 1))
    for array, h in first:
        start_in(array, h, 0)
    for array, h in first:
        local_in(array, h).wait()
        start_own(array, h, me)
    start_all_in(KEY, 0)
    start_all_in(VALUE, 0)
    for array, h in first:
        wait_in(array, h, 0)
        start_own(array, h, me ^ 1)
    for array, h in order[2:]:
        start_all_in(array, h)
    start_near(KEY, 0)
    pass_on(KEY, 0, 0)
    pass_on(VALUE, 0, 0)
    start_near(VALUE, 0)
    pass_on(KEY, 1, 0)
    pass_on(VALUE, 1, 0)
    pass_on(KEY, 0, 1)
    wait_all_in(QUERY, 0)
    turn(QUERY, 0)
    pass_on(KEY, 0, 3)
    forward(0, 0, 1)
    pass_on(KEY, 0, 2)
    forward(0, 0, 0)
    start_near(KEY, 1)
    pass_on(VALUE, 0, 1)
    forward(1, 0, 1)
    pass_on(VALUE, 0, 3)
    pass_on(VALUE, 0, 2)
    start_near(VALUE, 1)
    forward(1, 0, 0)
    pass_on(KEY, 1, 1)
    wait_all_in(GRAD, 0)
    turn(GRAD, 0)
    pass_on(KEY, 1, 3)
    wait_far(0, (0, 1))
    forward(2, 0, 1)
    pass_on(KEY, 1, 2)
    wait_far(0, (3, 2))
    forward(2, 0, 0)
    pass_on(VALUE, 1, 1)
    finish_forward(0)
    pass_on(VALUE, 1, 3)
    backward(2, 0, 0)
    pass_on(VALUE, 1, 2)
    send_far(0, 0)
    send_out(0, 0, 0)
    send_out(0, 0, 1)
    backward(2, 0, 1)
    send_far(0, 1)
    wait_all_in(QUERY, 1)
    turn(QUERY, 1)
    backward(1, 0, 0)
    backward(1, 0, 1)
    backward(0, 0, 0)
    backward(0, 0, 1)
    finish_queries(0)
    forward(0, 1, 1)
    reduce_near(0, 0, 0)
    forward(0, 1, 0)
    reduce_near(0, 0, 1)
    wait_all_in(GRAD, 1)
    turn(GRAD, 1)
    forward(1, 1, 1)
    reduce_near(0, 1, 0)
    forward(1, 1, 0)
    wait_far(1, (0, 1))
    forward(2, 1, 1)
    reduce_near(0, 1, 1)
    wait_far(1, (3, 2))
    forward(2, 1, 0)
    finish_forward(1)
    backward(2, 1, 0)
    send_far(1, 0)
    send_out(0, 1, 0)
    send_out(0, 1, 1)
    backward(2, 1, 1)
    send_far(1, 1)
    backward(1, 1, 0)
    finish_keys(0, 0, 0)
    reduce_near(1, 0, 0)
    backward(1, 1, 1)
    finish_keys(0, 0, 1)
    reduce_near(1, 0, 1)
    backward(0, 1, 0)
    finish_keys(0, 1, 0)
    reduce_near(1, 1, 0)
    backward(0, 1, 1)
    finish_queries(1)
    finish_keys(0, 1, 1)
    finish_keys(1, 0, 0)
    reduce_near(1, 1, 1)
    finish_keys(1, 0, 1)
    finish_keys(1, 1, 0)
    finish_keys(1, 1, 1)

    for array in range(4):
        for h in range(2):
            part = landing(array, h).at[pl.ds(0, 7 * ROWS)]
            pltpu.make_async_copy(part, part, in_send.at[array, h]).wait()
    for array in range(2):
        for h in range(2):
            for axis in range(2):
                for chip in range(4):
                    hop(axis, 0, array, h, chip).wait_send()
                    hop(axis, 1, array, h, chip).wait_send()
                for s in range(2):
                    far_copy(axis, array, h, s).wait_send()
                    near_copy(axis, array, h, s).wait_send()
    for array in range(4):
        for h in range(2):
            out_keep(array, h).wait()
            part = staged.at[array, h, pl.ds(0, 7 * ROWS)]
            pltpu.make_async_copy(part, part, out_send.at[array, h]).wait()
            pltpu.make_async_copy(part, part, out_recv.at[array, h]).wait()


def keep_kernel(in0, in1, in2, in3, out0, out1, out2, out3, done):
    copies = [
        pltpu.make_async_copy(src, dst, done.at[i])
        for i, (src, dst) in enumerate(((in0, out0), (in1, out1), (in2, out2), (in3, out3)))
    ]
    for copy in copies:
        copy.start()
    for copy in copies:
        copy.wait()


def body(queries, key_rows, value_rows, grad_out):
    dma = pltpu.SemaphoreType.DMA
    term = (2, 2, 2, 2, BLOCK, HEAD_DIM)
    shape = jax.ShapeDtypeStruct(queries.shape, BF16)
    results = pl.pallas_call(
        kernel,
        out_shape=[shape] * 4,
        in_specs=[pl.BlockSpec(memory_space=pl.ANY)] * 4,
        out_specs=[pl.BlockSpec(memory_space=pl.ANY)] * 4,
        scratch_shapes=[
            pltpu.VMEM((5, 2, 2, 2 * BLOCK, HEAD_DIM), BF16),
            pltpu.VMEM((2, 2, 2 * BLOCK, HEAD_DIM), BF16),
            pltpu.VMEM((2, 2, 2, HEAD_DIM, BLOCK), BF16),
            pltpu.VMEM((2, 6, 2, BLOCK, BLOCK), BF16),
            pltpu.VMEM((2, 6, 2, 1, BLOCK), F32),
            pltpu.VMEM((2, 2, 1, BLOCK), F32),
            pltpu.VMEM((2, 2, 1, BLOCK), F32),
            pltpu.VMEM((2, 2, HEAD_DIM, BLOCK), F32),
            pltpu.VMEM((2, 2, HEAD_DIM, BLOCK), F32),
            pltpu.VMEM((2, 2, 1, BLOCK), F32),
            pltpu.VMEM((2, 2, 2, BLOCK, HEAD_DIM), F32),
            pltpu.VMEM(term, F32),
            pltpu.VMEM(term, BF16),
            pltpu.VMEM(term, BF16),
            pltpu.VMEM(term, BF16),
            pltpu.VMEM(term, BF16),
            pltpu.VMEM((4, 2, 2 * BLOCK, HEAD_DIM), BF16),
            dma((4, 2)), dma((4, 2, 4)), dma((4, 2)),
            dma((2, 2, 2, 2, 4)), dma((2, 2, 2, 2, 4)),
            dma((2, 2, 2, 2)), dma((2, 2, 2, 2)), dma((2, 2, 2, 2)), dma((2, 2, 2, 2)),
            dma((4, 2)), dma((4, 2)), dma((4, 2)),
        ],
        compiler_params=pltpu.CompilerParams(
            collective_id=0, has_side_effects=True, vmem_limit_bytes=103 * 2 ** 19
        ),
        cost_estimate=pl.CostEstimate(
            flops=7 * 24 * 2 * BLOCK * BLOCK * HEAD_DIM, bytes_accessed=2 ** 22, transcendentals=24 * BLOCK * BLOCK
        ),
        name="butterfly_attention",
    )(queries, key_rows, value_rows, grad_out)
    return pl.pallas_call(
        keep_kernel,
        out_shape=[shape] * 4,
        in_specs=[pl.BlockSpec(memory_space=pl.ANY)] * 4,
        out_specs=[pl.BlockSpec(memory_space=pl.ANY)] * 4,
        scratch_shapes=[dma((4,))],
        compiler_params=pltpu.CompilerParams(vmem_limit_bytes=2 * 2 ** 20),
        name="keep_results",
    )(*results)


def solution(mesh):
    placed = P(("context", "ulysses"), None)
    return jax.shard_map(
        body, mesh=mesh, in_specs=(placed,) * 4, out_specs=(placed,) * 4, check_vma=False
    )
```

```python
import jax
import jax.numpy as jnp
from jax import lax
from jax.experimental import pallas as pl
from jax.experimental.pallas import tpu as pltpu
from jax.sharding import PartitionSpec as P

HEAD_DIM = 128
BLOCK = 512
ROWS = 128
F32 = jnp.float32
BF16 = jnp.bfloat16
SCALE = HEAD_DIM ** -0.5
EXP2_SCALE = SCALE * 1.4426950408889634
MESH = pl.DeviceIdType.MESH

KEY, VALUE, QUERY, GRAD = range(4)
GROUPS = ((0, 1), (2, 4), (3, 5))


def dot(a, b, ca, cb):
    return lax.dot_general(a, b, (((ca,), (cb,)), ((), ())), preferred_element_type=F32)


def kernel(
    q_in, k_in, v_in, g_in, out0, out1, out2, out3,
    kv, qg, qg_t, weights, peaks, run_peak, run_total, out_acc, query_acc, dots,
    acc, near, far_send, far_recv, near_send, near_recv, staged,
    in_send, in_recv, in_local, fwd_send, fwd_recv, far_ssem, far_rsem, near_ssem, near_rsem,
    out_send, out_recv, out_local,
):
    context = lax.axis_index("context")
    ulysses = lax.axis_index("ulysses")
    x = context // 8
    y = (context // 2) % 4
    z = (context % 2) * 2 + ulysses // 2
    core = ulysses % 2
    me = z * 2 + core

    def device(x, y, e):
        return {"context": x * 8 + y * 2 + e // 4, "ulysses": e % 4}

    def near_of(v):
        return v + 1 - 2 * (v % 2)

    def far_of(v):
        return 3 - v

    near_device = [device(near_of(x), y, me), device(x, near_of(y), me)]
    far_device = [device(far_of(x), y, me), device(x, far_of(y), me)]

    def remote(src, dst, ssem, rsem, to):
        return pltpu.make_async_remote_copy(
            src_ref=src, dst_ref=dst, send_sem=ssem, recv_sem=rsem, device_id=to, device_id_type=MESH
        )

    inputs = {KEY: k_in, VALUE: v_in, QUERY: q_in, GRAD: g_in}

    def landing(array, h):
        return kv.at[0, array, h] if array < 2 else qg.at[array - 2, h]

    def columns(e, h):
        return pl.ds(pl.multiple_of(e * 256 + h * 128, 128), 128)

    def rows_of(e):
        return pl.ds(pl.multiple_of(e * ROWS, ROWS), ROWS)

    order = [(KEY, 0), (VALUE, 0), (QUERY, 0), (KEY, 1), (VALUE, 1), (GRAD, 0), (QUERY, 1), (GRAD, 1)]

    def local_in(array, h):
        return pltpu.make_async_copy(
            inputs[array].at[:, columns(me, h)], landing(array, h).at[rows_of(me)], in_local.at[array, h]
        )

    for array, h in order:
        local_in(array, h).start()

    barrier = pltpu.get_barrier_semaphore()
    partners = [device(x, y, me ^ k) for k in range(1, 8)] + near_device + far_device
    for partner in partners:
        pl.semaphore_signal(barrier, inc=1, device_id=partner, device_id_type=MESH)
    pl.semaphore_wait(barrier, len(partners))

    def start_in(array, h, chip):
        for c in range(2):
            e = (z ^ chip) * 2 + (core ^ 1 if c == 0 else core)
            if chip or c == 0:
                remote(
                    inputs[array].at[:, columns(e, h)],
                    landing(array, h).at[rows_of(me)],
                    in_send.at[array, h],
                    in_recv.at[array, h, chip],
                    device(x, y, e),
                ).start()

    def wait_in(array, h, chip):
        rows = ROWS if chip == 0 else 2 * ROWS
        part = landing(array, h).at[pl.ds(0, rows)]
        pltpu.make_async_copy(part, part, in_recv.at[array, h, chip]).wait()

    z_hi = z // 2

    def at(i):
        return 1 - z_hi if i == 0 else z_hi

    def block_rows(s):
        return pl.ds(pl.multiple_of(s * BLOCK, BLOCK), BLOCK)

    def hop(axis, hop_at, array, h, chip):
        source = 0 if hop_at == 0 else 1 + 2 * axis
        rows = pl.ds(pl.multiple_of((z ^ chip) * 256, 256), 256)
        return remote(
            kv.at[source, array, h, rows],
            kv.at[1 + 2 * axis + hop_at, array, h, rows],
            fwd_send.at[axis, hop_at, array, h, chip],
            fwd_recv.at[axis, hop_at, array, h, chip],
            near_device[axis] if hop_at == 0 else far_device[axis],
        )

    def start_own(array, h, e):
        for axis in range(2):
            remote(
                kv.at[0, array, h, rows_of(e)],
                kv.at[1 + 2 * axis, array, h, rows_of(e)],
                fwd_send.at[axis, 0, array, h, 0],
                fwd_recv.at[axis, 0, array, h, 0],
                near_device[axis],
            ).start()

    def start_near(array, h, chip):
        wait_in(array, h, chip)
        for axis in range(2):
            hop(axis, 0, array, h, chip).start()

    def pass_on(array, h, chip):
        for axis in range(2):
            hop(axis, 0, array, h, chip).wait_recv()
            hop(axis, 1, array, h, chip).start()

    def wait_far(h, chips):
        for chip in chips:
            for array in range(2):
                for axis in range(2):
                    hop(axis, 1, array, h, chip).wait_recv()

    def turn(array, h, i):
        if i == 1:
            local_in(array, h).wait()
        for chip in (2, 3) if i == 0 else (0, 1):
            wait_in(array, h, chip)
        qg_t[array - 2, h, at(i)] = qg[array - 2, h, block_rows(at(i)), :].T

    def pair(j, h, s):
        source = 0 if j < 2 else j - 1
        rows = block_rows(1 - s if j == 1 else s)
        return kv[source, 0, h, rows, :], kv[source, 1, h, rows, :]

    def forward(group, h, i):
        s = at(i)
        pairs = [pair(j, h, s) for j in GROUPS[group]]
        scores = [dot(keys, qg_t[0, h, s], 1, 0) for keys, _ in pairs]
        peak = jnp.maximum(*[jnp.max(each, axis=0, keepdims=True) for each in scores])
        total, part = 0.0, 0.0
        for j, each, (_, values) in zip(GROUPS[group], scores, pairs):
            shifted = jnp.exp2((each - peak) * EXP2_SCALE)
            total = total + jnp.sum(shifted, axis=0, keepdims=True)
            low = shifted.astype(BF16)
            weights[h, j, s] = low
            part = part + dot(values, low, 0, 0)
        peaks[h, group, s] = peak
        if group == 0:
            run_peak[h, s] = peak
            run_total[h, s] = total
            out_acc[h, s] = part
        else:
            old = run_peak[h, s]
            joined = jnp.maximum(old, peak)
            keep = jnp.exp2((old - joined) * EXP2_SCALE)
            fresh = jnp.exp2((peak - joined) * EXP2_SCALE)
            run_peak[h, s] = joined
            run_total[h, s] = run_total[h, s] * keep + total * fresh
            out_acc[h, s] = out_acc[h, s] * keep + part * fresh

    outs = [out0, out1, out2, out3]

    def out_copy(array, h, e):
        return remote(
            staged.at[array, h, rows_of(e)],
            outs[array].at[:, columns(me, h)],
            out_send.at[array, h],
            out_recv.at[array, h],
            device(x, y, e),
        )

    def out_keep(array, h):
        return pltpu.make_async_copy(
            staged.at[array, h, rows_of(me)], outs[array].at[:, columns(me, h)], out_local.at[array, h]
        )

    def send_out(array, h, i):
        for chip in (2, 3) if i == 0 else (1, 0):
            for c in range(2):
                e = (z ^ chip) * 2 + (core ^ 1 if c == 0 else core)
                if chip or c == 0:
                    out_copy(array, h, e).start()
        if i == 1:
            out_keep(array, h).start()

    def finish_forward(h, i):
        s = at(i)
        attended = (out_acc[h, s] / run_total[h, s]).astype(BF16)
        dots[h, s] = jnp.sum(attended.astype(F32) * qg_t[1, h, s].astype(F32), axis=0, keepdims=True)
        staged[0, h, block_rows(s)] = attended.T

    def finish_queries(h, i):
        s = at(i)
        staged[1, h, block_rows(s)] = query_acc[h, s].astype(BF16).T
        send_out(1, h, i)

    def far_copy(axis, array, h, s):
        return remote(
            far_send.at[axis, array, h, s], far_recv.at[axis, array, h, s],
            far_ssem.at[axis, array, h, s], far_rsem.at[axis, array, h, s], far_device[axis],
        )

    def near_copy(axis, array, h, s):
        return remote(
            near_send.at[axis, array, h, s], near_recv.at[axis, array, h, s],
            near_ssem.at[axis, array, h, s], near_rsem.at[axis, array, h, s], near_device[axis],
        )

    def backward(group, h, i):
        s = at(i)
        factor = jnp.exp2((peaks[h, group, s] - run_peak[h, s]) * EXP2_SCALE) / run_total[h, s]
        scaled = factor * SCALE
        grads = qg_t[1, h, s]
        grads_scaled = (grads.astype(F32) * factor).astype(BF16)
        queries_scaled = (qg_t[0, h, s].astype(F32) * scaled).astype(BF16)
        query_part = 0.0
        for j in GROUPS[group]:
            axis = (j - 2) // 2
            keys, values = pair(j, h, s)
            low = weights[h, j, s]
            grad_probs = dot(values, grads, 1, 0)
            grad_scores = (low.astype(F32) * (grad_probs - dots[h, s])).astype(BF16)
            query_part = query_part + dot(keys, grad_scores, 0, 0)
            value_term = dot(low, grads_scaled, 1, 1)
            key_term = dot(grad_scores, queries_scaled, 1, 1)
            for array, term in ((0, key_term), (1, value_term)):
                if group == 2:
                    far_send[axis, array, h, s] = term.astype(BF16)
                elif group == 1:
                    near[axis, array, h, s] = term
                elif i == 1 - h:
                    acc[array, h, s if j == 0 else 1 - s] = term
                else:
                    place = s if j == 0 else 1 - s
                    acc[array, h, place] = acc[array, h, place] + term
        if group == 2:
            query_acc[h, s] = query_part * scaled
        else:
            query_acc[h, s] = query_acc[h, s] + query_part * scaled

    def send_far(h, i):
        for array in range(2):
            for axis in range(2):
                far_copy(axis, array, h, at(i)).start()

    def reduce_near(h, i, array):
        s = at(i)
        for axis in range(2):
            far_copy(axis, array, h, s).wait_recv()
            near_send[axis, array, h, s] = (
                near[axis, array, h, s] + far_recv[axis, array, h, s].astype(F32)
            ).astype(BF16)
            near_copy(axis, array, h, s).start()

    def finish_keys(h, i, array):
        s = at(i)
        total = acc[array, h, s]
        for axis in range(2):
            near_copy(axis, array, h, s).wait_recv()
            total = total + near_recv[axis, array, h, s].astype(F32)
        staged[2 + array, h, block_rows(s)] = total.astype(BF16)
        send_out(2 + array, h, i)

    first = ((KEY, 0), (VALUE, 0), (KEY, 1), (VALUE, 1))
    for array, h in first:
        start_in(array, h, 0)
    for array, h in first:
        local_in(array, h).wait()
        start_own(array, h, me)
    for chip in (1, 2, 3):
        start_in(KEY, 0, chip)
    for chip in (1, 2, 3):
        start_in(VALUE, 0, chip)
    for array, h in first:
        wait_in(array, h, 0)
        start_own(array, h, me ^ 1)
    for array, h, chips in (
        (QUERY, 0, (0, 1, 2, 3)), (GRAD, 0, (0, 1)), (KEY, 1, (2, 3, 1)), (VALUE, 1, (2, 3, 1)),
        (GRAD, 0, (2, 3)), (QUERY, 1, (2, 3, 1, 0)), (GRAD, 1, (2, 3, 1, 0)),
    ):
        for chip in chips:
            start_in(array, h, chip)

    start_near(KEY, 0, 1)
    pass_on(KEY, 0, 0)
    pass_on(VALUE, 0, 0)
    start_near(VALUE, 0, 1)
    start_near(KEY, 0, 3)
    start_near(KEY, 0, 2)
    pass_on(KEY, 1, 0)
    pass_on(VALUE, 1, 0)
    start_near(VALUE, 0, 3)
    start_near(VALUE, 0, 2)
    pass_on(KEY, 0, 1)
    turn(QUERY, 0, 1)
    pass_on(VALUE, 0, 1)
    forward(0, 0, 1)
    pass_on(KEY, 0, 3)
    forward(1, 0, 1)
    pass_on(KEY, 0, 2)
    turn(GRAD, 0, 1)
    start_near(KEY, 1, 3)
    start_near(KEY, 1, 2)
    pass_on(VALUE, 0, 3)
    wait_far(0, (0, 1))
    forward(2, 0, 1)
    pass_on(VALUE, 0, 2)
    finish_forward(0, 1)
    send_out(0, 0, 1)
    start_near(VALUE, 1, 3)
    start_near(VALUE, 1, 2)
    backward(2, 0, 1)
    pass_on(KEY, 1, 3)
    start_near(KEY, 1, 1)
    start_near(VALUE, 1, 1)
    backward(1, 0, 1)
    pass_on(KEY, 1, 2)
    turn(QUERY, 0, 0)
    forward(0, 0, 0)
    pass_on(VALUE, 1, 3)
    forward(1, 0, 0)
    pass_on(VALUE, 1, 2)
    wait_far(0, (3, 2))
    forward(2, 0, 0)
    pass_on(KEY, 1, 1)
    turn(GRAD, 0, 0)
    finish_forward(0, 0)
    send_out(0, 0, 0)
    pass_on(VALUE, 1, 1)
    send_far(0, 1)
    backward(2, 0, 0)
    send_far(0, 0)
    backward(0, 0, 1)
    backward(1, 0, 0)
    backward(0, 0, 0)
    finish_queries(0, 1)
    finish_queries(0, 0)
    turn(QUERY, 1, 1)
    turn(QUERY, 1, 0)
    forward(0, 1, 0)
    reduce_near(0, 1, 0)
    forward(1, 1, 0)
    turn(GRAD, 1, 1)
    turn(GRAD, 1, 0)
    wait_far(1, (3, 2))
    forward(2, 1, 0)
    reduce_near(0, 1, 1)
    finish_forward(1, 0)
    backward(2, 1, 0)
    send_far(1, 0)
    send_out(0, 1, 0)
    forward(0, 1, 1)
    reduce_near(0, 0, 0)
    forward(1, 1, 1)
    wait_far(1, (0, 1))
    forward(2, 1, 1)
    finish_forward(1, 1)
    backward(2, 1, 1)
    send_far(1, 1)
    reduce_near(0, 0, 1)
    send_out(0, 1, 1)
    finish_keys(0, 1, 0)
    backward(1, 1, 0)
    reduce_near(1, 0, 0)
    finish_keys(0, 1, 1)
    backward(1, 1, 1)
    reduce_near(1, 0, 1)
    finish_keys(0, 0, 0)
    backward(0, 1, 0)
    finish_queries(1, 0)
    finish_keys(0, 0, 1)
    reduce_near(1, 1, 0)
    backward(0, 1, 1)
    finish_queries(1, 1)
    finish_keys(1, 0, 0)
    reduce_near(1, 1, 1)
    finish_keys(1, 0, 1)
    finish_keys(1, 1, 0)
    finish_keys(1, 1, 1)

    for array in range(4):
        for h in range(2):
            part = landing(array, h).at[pl.ds(0, 7 * ROWS)]
            pltpu.make_async_copy(part, part, in_send.at[array, h]).wait()
    for array in range(2):
        for h in range(2):
            for axis in range(2):
                for chip in range(4):
                    hop(axis, 0, array, h, chip).wait_send()
                    hop(axis, 1, array, h, chip).wait_send()
                for s in range(2):
                    far_copy(axis, array, h, s).wait_send()
                    near_copy(axis, array, h, s).wait_send()
    for array in range(4):
        for h in range(2):
            out_keep(array, h).wait()
            part = staged.at[array, h, pl.ds(0, 7 * ROWS)]
            pltpu.make_async_copy(part, part, out_send.at[array, h]).wait()
            pltpu.make_async_copy(part, part, out_recv.at[array, h]).wait()


def keep_kernel(in0, in1, in2, in3, out0, out1, out2, out3, done):
    copies = [
        pltpu.make_async_copy(src, dst, done.at[i])
        for i, (src, dst) in enumerate(((in0, out0), (in1, out1), (in2, out2), (in3, out3)))
    ]
    for copy in copies:
        copy.start()
    for copy in copies:
        copy.wait()


def body(queries, key_rows, value_rows, grad_out):
    dma = pltpu.SemaphoreType.DMA
    term = (2, 2, 2, 2, BLOCK, HEAD_DIM)
    shape = jax.ShapeDtypeStruct(queries.shape, BF16)
    results = pl.pallas_call(
        kernel,
        out_shape=[shape] * 4,
        in_specs=[pl.BlockSpec(memory_space=pl.ANY)] * 4,
        out_specs=[pl.BlockSpec(memory_space=pl.ANY)] * 4,
        scratch_shapes=[
            pltpu.VMEM((5, 2, 2, 2 * BLOCK, HEAD_DIM), BF16),
            pltpu.VMEM((2, 2, 2 * BLOCK, HEAD_DIM), BF16),
            pltpu.VMEM((2, 2, 2, HEAD_DIM, BLOCK), BF16),
            pltpu.VMEM((2, 6, 2, BLOCK, BLOCK), BF16),
            pltpu.VMEM((2, 6, 2, 1, BLOCK), F32),
            pltpu.VMEM((2, 2, 1, BLOCK), F32),
            pltpu.VMEM((2, 2, 1, BLOCK), F32),
            pltpu.VMEM((2, 2, HEAD_DIM, BLOCK), F32),
            pltpu.VMEM((2, 2, HEAD_DIM, BLOCK), F32),
            pltpu.VMEM((2, 2, 1, BLOCK), F32),
            pltpu.VMEM((2, 2, 2, BLOCK, HEAD_DIM), F32),
            pltpu.VMEM(term, F32),
            pltpu.VMEM(term, BF16),
            pltpu.VMEM(term, BF16),
            pltpu.VMEM(term, BF16),
            pltpu.VMEM(term, BF16),
            pltpu.VMEM((4, 2, 2 * BLOCK, HEAD_DIM), BF16),
            dma((4, 2)), dma((4, 2, 4)), dma((4, 2)),
            dma((2, 2, 2, 2, 4)), dma((2, 2, 2, 2, 4)),
            dma((2, 2, 2, 2)), dma((2, 2, 2, 2)), dma((2, 2, 2, 2)), dma((2, 2, 2, 2)),
            dma((4, 2)), dma((4, 2)), dma((4, 2)),
        ],
        compiler_params=pltpu.CompilerParams(
            collective_id=0, has_side_effects=True, vmem_limit_bytes=103 * 2 ** 19
        ),
        cost_estimate=pl.CostEstimate(
            flops=7 * 24 * 2 * BLOCK * BLOCK * HEAD_DIM, bytes_accessed=2 ** 22, transcendentals=24 * BLOCK * BLOCK
        ),
        name="butterfly_attention",
    )(queries, key_rows, value_rows, grad_out)
    return pl.pallas_call(
        keep_kernel,
        out_shape=[shape] * 4,
        in_specs=[pl.BlockSpec(memory_space=pl.ANY)] * 4,
        out_specs=[pl.BlockSpec(memory_space=pl.ANY)] * 4,
        scratch_shapes=[dma((4,))],
        compiler_params=pltpu.CompilerParams(vmem_limit_bytes=2 * 2 ** 20),
        name="keep_results",
    )(*results)


def solution(mesh):
    placed = P(("context", "ulysses"), None)
    return jax.shard_map(
        body, mesh=mesh, in_specs=(placed,) * 4, out_specs=(placed,) * 4, check_vma=False
    )
```

```python
import jax
import jax.numpy as jnp
from jax import lax
from jax.experimental import pallas as pl
from jax.experimental.pallas import tpu as pltpu
from jax.sharding import PartitionSpec as P

HEAD_DIM = 128
BLOCK = 512
ROWS = 128
F32 = jnp.float32
BF16 = jnp.bfloat16
SCALE = HEAD_DIM ** -0.5
EXP2_SCALE = SCALE * 1.4426950408889634
MESH = pl.DeviceIdType.MESH

KEY, VALUE, QUERY, GRAD = range(4)
GROUPS = ((0, 1), (2, 4), (3, 5))


def dot(a, b, ca, cb):
    return lax.dot_general(a, b, (((ca,), (cb,)), ((), ())), preferred_element_type=F32)


def kernel(
    q_in, k_in, v_in, g_in, out0, out1, out2, out3,
    kv, qg, qg_t, weights, peaks, run_peak, run_total, out_acc, query_acc, dots,
    acc, near, far_send, far_recv, near_send, near_recv, staged,
    in_send, in_recv, in_local, fwd_send, fwd_recv, far_ssem, far_rsem, near_ssem, near_rsem,
    out_send, out_recv, out_local,
):
    context = lax.axis_index("context")
    ulysses = lax.axis_index("ulysses")
    x = context // 8
    y = (context // 2) % 4
    z = (context % 2) * 2 + ulysses // 2
    core = ulysses % 2
    me = z * 2 + core

    def device(x, y, e):
        return {"context": x * 8 + y * 2 + e // 4, "ulysses": e % 4}

    def near_of(v):
        return v + 1 - 2 * (v % 2)

    def far_of(v):
        return 3 - v

    near_device = [device(near_of(x), y, me), device(x, near_of(y), me)]
    far_device = [device(far_of(x), y, me), device(x, far_of(y), me)]

    def remote(src, dst, ssem, rsem, to):
        return pltpu.make_async_remote_copy(
            src_ref=src, dst_ref=dst, send_sem=ssem, recv_sem=rsem, device_id=to, device_id_type=MESH
        )

    inputs = {KEY: k_in, VALUE: v_in, QUERY: q_in, GRAD: g_in}

    def landing(array, h):
        return kv.at[0, array, h] if array < 2 else qg.at[array - 2, h]

    def columns(e, h):
        return pl.ds(pl.multiple_of(e * 256 + h * 128, 128), 128)

    def rows_of(e):
        return pl.ds(pl.multiple_of(e * ROWS, ROWS), ROWS)

    order = [(KEY, 0), (VALUE, 0), (QUERY, 0), (KEY, 1), (VALUE, 1), (GRAD, 0), (QUERY, 1), (GRAD, 1)]

    def local_in(array, h):
        return pltpu.make_async_copy(
            inputs[array].at[:, columns(me, h)], landing(array, h).at[rows_of(me)], in_local.at[array, h]
        )

    for array, h in order:
        local_in(array, h).start()

    barrier = pltpu.get_barrier_semaphore()
    partners = [device(x, y, me ^ k) for k in range(1, 8)] + near_device + far_device
    for partner in partners:
        pl.semaphore_signal(barrier, inc=1, device_id=partner, device_id_type=MESH)
    pl.semaphore_wait(barrier, len(partners))

    def start_in(array, h, chip):
        for c in range(2):
            e = (z ^ chip) * 2 + (core ^ 1 if c == 0 else core)
            if chip or c == 0:
                remote(
                    inputs[array].at[:, columns(e, h)],
                    landing(array, h).at[rows_of(me)],
                    in_send.at[array, h],
                    in_recv.at[array, h, chip],
                    device(x, y, e),
                ).start()

    def wait_in(array, h, chip):
        rows = ROWS if chip == 0 else 2 * ROWS
        part = landing(array, h).at[pl.ds(0, rows)]
        pltpu.make_async_copy(part, part, in_recv.at[array, h, chip]).wait()

    z_hi = z // 2

    def at(i):
        return 1 - z_hi if i == 0 else z_hi

    def block_rows(s):
        return pl.ds(pl.multiple_of(s * BLOCK, BLOCK), BLOCK)

    def hop(axis, hop_at, array, h, chip):
        source = 0 if hop_at == 0 else 1 + 2 * axis
        rows = pl.ds(pl.multiple_of((z ^ chip) * 256, 256), 256)
        return remote(
            kv.at[source, array, h, rows],
            kv.at[1 + 2 * axis + hop_at, array, h, rows],
            fwd_send.at[axis, hop_at, array, h, chip],
            fwd_recv.at[axis, hop_at, array, h, chip],
            near_device[axis] if hop_at == 0 else far_device[axis],
        )

    def start_own(array, h, e):
        for axis in range(2):
            remote(
                kv.at[0, array, h, rows_of(e)],
                kv.at[1 + 2 * axis, array, h, rows_of(e)],
                fwd_send.at[axis, 0, array, h, 0],
                fwd_recv.at[axis, 0, array, h, 0],
                near_device[axis],
            ).start()

    def start_near(array, h, chip):
        wait_in(array, h, chip)
        for axis in range(2):
            hop(axis, 0, array, h, chip).start()

    def pass_on(array, h, chip):
        for axis in range(2):
            hop(axis, 0, array, h, chip).wait_recv()
            hop(axis, 1, array, h, chip).start()

    def wait_far(h, chips):
        for chip in chips:
            for array in range(2):
                for axis in range(2):
                    hop(axis, 1, array, h, chip).wait_recv()

    def turn(array, h, i):
        if i == 1:
            local_in(array, h).wait()
        for chip in (2, 3) if i == 0 else (0, 1):
            wait_in(array, h, chip)
        qg_t[array - 2, h, at(i)] = qg[array - 2, h, block_rows(at(i)), :].T

    def pair(j, h, s):
        source = 0 if j < 2 else j - 1
        rows = block_rows(1 - s if j == 1 else s)
        return kv[source, 0, h, rows, :], kv[source, 1, h, rows, :]

    def forward(group, h, i):
        s = at(i)
        pairs = [pair(j, h, s) for j in GROUPS[group]]
        scores = [dot(keys, qg_t[0, h, s], 1, 0) for keys, _ in pairs]
        peak = jnp.maximum(*[jnp.max(each, axis=0, keepdims=True) for each in scores])
        total, part = 0.0, 0.0
        for j, each, (_, values) in zip(GROUPS[group], scores, pairs):
            shifted = jnp.exp2((each - peak) * EXP2_SCALE)
            total = total + jnp.sum(shifted, axis=0, keepdims=True)
            low = shifted.astype(BF16)
            weights[h, j, s] = low
            part = part + dot(values, low, 0, 0)
        peaks[h, group, s] = peak
        if group == 0:
            run_peak[h, s] = peak
            run_total[h, s] = total
            out_acc[h, s] = part
        else:
            old = run_peak[h, s]
            joined = jnp.maximum(old, peak)
            keep = jnp.exp2((old - joined) * EXP2_SCALE)
            fresh = jnp.exp2((peak - joined) * EXP2_SCALE)
            run_peak[h, s] = joined
            run_total[h, s] = run_total[h, s] * keep + total * fresh
            out_acc[h, s] = out_acc[h, s] * keep + part * fresh

    outs = [out0, out1, out2, out3]

    def out_copy(array, h, e):
        return remote(
            staged.at[array, h, rows_of(e)],
            outs[array].at[:, columns(me, h)],
            out_send.at[array, h],
            out_recv.at[array, h],
            device(x, y, e),
        )

    def out_keep(array, h):
        return pltpu.make_async_copy(
            staged.at[array, h, rows_of(me)], outs[array].at[:, columns(me, h)], out_local.at[array, h]
        )

    def send_out(array, h, i):
        for chip in (2, 3) if i == 0 else (1, 0):
            for c in range(2):
                e = (z ^ chip) * 2 + (core ^ 1 if c == 0 else core)
                if chip or c == 0:
                    out_copy(array, h, e).start()
        if i == 1:
            out_keep(array, h).start()

    def finish_forward(h, i):
        s = at(i)
        attended = (out_acc[h, s] / run_total[h, s]).astype(BF16)
        dots[h, s] = jnp.sum(attended.astype(F32) * qg_t[1, h, s].astype(F32), axis=0, keepdims=True)
        staged[0, h, block_rows(s)] = attended.T

    def finish_queries(h, i):
        s = at(i)
        staged[1, h, block_rows(s)] = query_acc[h, s].astype(BF16).T
        send_out(1, h, i)

    def far_copy(axis, array, h, s):
        return remote(
            far_send.at[axis, array, h, s], far_recv.at[axis, array, h, s],
            far_ssem.at[axis, array, h, s], far_rsem.at[axis, array, h, s], far_device[axis],
        )

    def near_copy(axis, array, h, s):
        return remote(
            near_send.at[axis, array, h, s], near_recv.at[axis, array, h, s],
            near_ssem.at[axis, array, h, s], near_rsem.at[axis, array, h, s], near_device[axis],
        )

    def backward(group, h, i):
        s = at(i)
        factor = jnp.exp2((peaks[h, group, s] - run_peak[h, s]) * EXP2_SCALE) / run_total[h, s]
        scaled = factor * SCALE
        grads = qg_t[1, h, s]
        grads_scaled = (grads.astype(F32) * factor).astype(BF16)
        queries_scaled = (qg_t[0, h, s].astype(F32) * scaled).astype(BF16)
        query_part = 0.0
        for j in GROUPS[group]:
            axis = (j - 2) // 2
            keys, values = pair(j, h, s)
            low = weights[h, j, s]
            grad_probs = dot(values, grads, 1, 0)
            grad_scores = (low.astype(F32) * (grad_probs - dots[h, s])).astype(BF16)
            query_part = query_part + dot(keys, grad_scores, 0, 0)
            value_term = dot(low, grads_scaled, 1, 1)
            key_term = dot(grad_scores, queries_scaled, 1, 1)
            for array, term in ((0, key_term), (1, value_term)):
                if group == 2:
                    far_send[axis, array, h, s] = term.astype(BF16)
                elif group == 1:
                    near[axis, array, h, s] = term
                elif i == 1 - h:
                    acc[array, h, s if j == 0 else 1 - s] = term
                else:
                    place = s if j == 0 else 1 - s
                    acc[array, h, place] = acc[array, h, place] + term
        if group == 2:
            query_acc[h, s] = query_part * scaled
        else:
            query_acc[h, s] = query_acc[h, s] + query_part * scaled

    def send_far(h, i):
        for array in range(2):
            for axis in range(2):
                far_copy(axis, array, h, at(i)).start()

    def reduce_near(h, i, array):
        s = at(i)
        for axis in range(2):
            far_copy(axis, array, h, s).wait_recv()
            near_send[axis, array, h, s] = (
                near[axis, array, h, s] + far_recv[axis, array, h, s].astype(F32)
            ).astype(BF16)
            near_copy(axis, array, h, s).start()

    def finish_keys(h, i, array):
        s = at(i)
        total = acc[array, h, s]
        for axis in range(2):
            near_copy(axis, array, h, s).wait_recv()
            total = total + near_recv[axis, array, h, s].astype(F32)
        staged[2 + array, h, block_rows(s)] = total.astype(BF16)
        send_out(2 + array, h, i)

    first = ((KEY, 0), (VALUE, 0), (KEY, 1), (VALUE, 1))
    for array, h in first:
        start_in(array, h, 0)
    for array, h in first:
        local_in(array, h).wait()
        start_own(array, h, me)
    for chip in (1, 2, 3):
        start_in(KEY, 0, chip)
    for chip in (1, 2, 3):
        start_in(VALUE, 0, chip)
    for array, h in first:
        wait_in(array, h, 0)
        start_own(array, h, me ^ 1)
    for array, h, chips in (
        (QUERY, 0, (0, 1, 2, 3)), (GRAD, 0, (0, 1)), (KEY, 1, (2, 3, 1)), (VALUE, 1, (2, 3, 1)),
        (GRAD, 0, (2, 3)), (QUERY, 1, (2, 3, 1, 0)), (GRAD, 1, (2, 3, 1, 0)),
    ):
        for chip in chips:
            start_in(array, h, chip)

    start_near(KEY, 0, 1)
    pass_on(KEY, 0, 0)
    pass_on(VALUE, 0, 0)
    start_near(VALUE, 0, 1)
    start_near(KEY, 0, 3)
    start_near(KEY, 0, 2)
    pass_on(KEY, 1, 0)
    pass_on(VALUE, 1, 0)
    start_near(VALUE, 0, 3)
    start_near(VALUE, 0, 2)
    pass_on(KEY, 0, 1)
    turn(QUERY, 0, 1)
    pass_on(VALUE, 0, 1)
    forward(0, 0, 1)
    pass_on(KEY, 0, 3)
    forward(1, 0, 1)
    pass_on(KEY, 0, 2)
    turn(GRAD, 0, 1)
    start_near(KEY, 1, 3)
    start_near(KEY, 1, 2)
    pass_on(VALUE, 0, 3)
    wait_far(0, (0, 1))
    forward(2, 0, 1)
    pass_on(VALUE, 0, 2)
    finish_forward(0, 1)
    send_out(0, 0, 1)
    backward(2, 0, 1)
    start_near(KEY, 1, 1)
    start_near(VALUE, 1, 3)
    start_near(VALUE, 1, 2)
    pass_on(KEY, 1, 3)
    backward(1, 0, 1)
    start_near(VALUE, 1, 1)
    pass_on(KEY, 1, 2)
    backward(0, 0, 1)
    turn(QUERY, 0, 0)
    pass_on(VALUE, 1, 3)
    forward(0, 0, 0)
    forward(1, 0, 0)
    pass_on(VALUE, 1, 2)
    wait_far(0, (3, 2))
    forward(2, 0, 0)
    turn(GRAD, 0, 0)
    finish_forward(0, 0)
    pass_on(KEY, 1, 1)
    send_far(0, 1)
    send_out(0, 0, 0)
    backward(2, 0, 0)
    pass_on(VALUE, 1, 1)
    send_far(0, 0)
    backward(1, 0, 0)
    backward(0, 0, 0)
    finish_queries(0, 1)
    finish_queries(0, 0)
    turn(QUERY, 1, 1)
    turn(QUERY, 1, 0)
    forward(0, 1, 0)
    reduce_near(0, 1, 0)
    forward(1, 1, 0)
    turn(GRAD, 1, 1)
    turn(GRAD, 1, 0)
    wait_far(1, (3, 2))
    forward(2, 1, 0)
    reduce_near(0, 1, 1)
    finish_forward(1, 0)
    backward(2, 1, 0)
    send_far(1, 0)
    send_out(0, 1, 0)
    forward(0, 1, 1)
    reduce_near(0, 0, 0)
    forward(1, 1, 1)
    wait_far(1, (0, 1))
    forward(2, 1, 1)
    finish_forward(1, 1)
    backward(2, 1, 1)
    send_far(1, 1)
    reduce_near(0, 0, 1)
    send_out(0, 1, 1)
    finish_keys(0, 1, 0)
    backward(1, 1, 0)
    reduce_near(1, 0, 0)
    finish_keys(0, 1, 1)
    backward(1, 1, 1)
    reduce_near(1, 0, 1)
    finish_keys(0, 0, 0)
    backward(0, 1, 0)
    finish_queries(1, 0)
    finish_keys(0, 0, 1)
    reduce_near(1, 1, 0)
    backward(0, 1, 1)
    finish_queries(1, 1)
    finish_keys(1, 0, 0)
    reduce_near(1, 1, 1)
    finish_keys(1, 0, 1)
    finish_keys(1, 1, 0)
    finish_keys(1, 1, 1)

    for array in range(4):
        for h in range(2):
            part = landing(array, h).at[pl.ds(0, 7 * ROWS)]
            pltpu.make_async_copy(part, part, in_send.at[array, h]).wait()
    for array in range(2):
        for h in range(2):
            for axis in range(2):
                for chip in range(4):
                    hop(axis, 0, array, h, chip).wait_send()
                    hop(axis, 1, array, h, chip).wait_send()
                for s in range(2):
                    far_copy(axis, array, h, s).wait_send()
                    near_copy(axis, array, h, s).wait_send()
    for array in range(4):
        for h in range(2):
            out_keep(array, h).wait()
            part = staged.at[array, h, pl.ds(0, 7 * ROWS)]
            pltpu.make_async_copy(part, part, out_send.at[array, h]).wait()
            pltpu.make_async_copy(part, part, out_recv.at[array, h]).wait()


def keep_kernel(in0, in1, in2, in3, out0, out1, out2, out3, done):
    copies = [
        pltpu.make_async_copy(src, dst, done.at[i])
        for i, (src, dst) in enumerate(((in0, out0), (in1, out1), (in2, out2), (in3, out3)))
    ]
    for copy in copies:
        copy.start()
    for copy in copies:
        copy.wait()


def body(queries, key_rows, value_rows, grad_out):
    dma = pltpu.SemaphoreType.DMA
    term = (2, 2, 2, 2, BLOCK, HEAD_DIM)
    shape = jax.ShapeDtypeStruct(queries.shape, BF16)
    results = pl.pallas_call(
        kernel,
        out_shape=[shape] * 4,
        in_specs=[pl.BlockSpec(memory_space=pl.ANY)] * 4,
        out_specs=[pl.BlockSpec(memory_space=pl.ANY)] * 4,
        scratch_shapes=[
            pltpu.VMEM((5, 2, 2, 2 * BLOCK, HEAD_DIM), BF16),
            pltpu.VMEM((2, 2, 2 * BLOCK, HEAD_DIM), BF16),
            pltpu.VMEM((2, 2, 2, HEAD_DIM, BLOCK), BF16),
            pltpu.VMEM((2, 6, 2, BLOCK, BLOCK), BF16),
            pltpu.VMEM((2, 6, 2, 1, BLOCK), F32),
            pltpu.VMEM((2, 2, 1, BLOCK), F32),
            pltpu.VMEM((2, 2, 1, BLOCK), F32),
            pltpu.VMEM((2, 2, HEAD_DIM, BLOCK), F32),
            pltpu.VMEM((2, 2, HEAD_DIM, BLOCK), F32),
            pltpu.VMEM((2, 2, 1, BLOCK), F32),
            pltpu.VMEM((2, 2, 2, BLOCK, HEAD_DIM), F32),
            pltpu.VMEM(term, F32),
            pltpu.VMEM(term, BF16),
            pltpu.VMEM(term, BF16),
            pltpu.VMEM(term, BF16),
            pltpu.VMEM(term, BF16),
            pltpu.VMEM((4, 2, 2 * BLOCK, HEAD_DIM), BF16),
            dma((4, 2)), dma((4, 2, 4)), dma((4, 2)),
            dma((2, 2, 2, 2, 4)), dma((2, 2, 2, 2, 4)),
            dma((2, 2, 2, 2)), dma((2, 2, 2, 2)), dma((2, 2, 2, 2)), dma((2, 2, 2, 2)),
            dma((4, 2)), dma((4, 2)), dma((4, 2)),
        ],
        compiler_params=pltpu.CompilerParams(
            collective_id=0, has_side_effects=True, vmem_limit_bytes=103 * 2 ** 19
        ),
        cost_estimate=pl.CostEstimate(
            flops=7 * 24 * 2 * BLOCK * BLOCK * HEAD_DIM, bytes_accessed=2 ** 22, transcendentals=24 * BLOCK * BLOCK
        ),
        name="butterfly_attention",
    )(queries, key_rows, value_rows, grad_out)
    return pl.pallas_call(
        keep_kernel,
        out_shape=[shape] * 4,
        in_specs=[pl.BlockSpec(memory_space=pl.ANY)] * 4,
        out_specs=[pl.BlockSpec(memory_space=pl.ANY)] * 4,
        scratch_shapes=[dma((4,))],
        compiler_params=pltpu.CompilerParams(vmem_limit_bytes=2 * 2 ** 20),
        name="keep_results",
    )(*results)


def solution(mesh):
    placed = P(("context", "ulysses"), None)
    return jax.shard_map(
        body, mesh=mesh, in_specs=(placed,) * 4, out_specs=(placed,) * 4, check_vma=False
    )
```

```python
import jax
import jax.numpy as jnp
from jax import lax
from jax.experimental import pallas as pl
from jax.experimental.pallas import tpu as pltpu
from jax.sharding import PartitionSpec as P

HEAD_DIM = 128
BLOCK = 512
ROWS = 128
F32 = jnp.float32
BF16 = jnp.bfloat16
SCALE = HEAD_DIM ** -0.5
EXP2_SCALE = SCALE * 1.4426950408889634
MESH = pl.DeviceIdType.MESH

KEY, VALUE, QUERY, GRAD = range(4)
GROUPS = ((0, 1), (2, 4), (3, 5))


def dot(a, b, ca, cb):
    return lax.dot_general(a, b, (((ca,), (cb,)), ((), ())), preferred_element_type=F32)


def kernel(
    q_in, k_in, v_in, g_in, out0, out1, out2, out3,
    kv, qg, qg_t, weights, peaks, run_peak, run_total, out_acc, query_acc, dots,
    acc, near, far_send, far_recv, near_send, near_recv, staged,
    in_send, in_recv, in_local, fwd_send, fwd_recv, far_ssem, far_rsem, near_ssem, near_rsem,
    out_send, out_recv, out_local,
):
    context = lax.axis_index("context")
    ulysses = lax.axis_index("ulysses")
    x = context // 8
    y = (context // 2) % 4
    z = (context % 2) * 2 + ulysses // 2
    core = ulysses % 2
    me = z * 2 + core

    def device(x, y, e):
        return {"context": x * 8 + y * 2 + e // 4, "ulysses": e % 4}

    def near_of(v):
        return v + 1 - 2 * (v % 2)

    def far_of(v):
        return 3 - v

    near_device = [device(near_of(x), y, me), device(x, near_of(y), me)]
    far_device = [device(far_of(x), y, me), device(x, far_of(y), me)]

    def remote(src, dst, ssem, rsem, to):
        return pltpu.make_async_remote_copy(
            src_ref=src, dst_ref=dst, send_sem=ssem, recv_sem=rsem, device_id=to, device_id_type=MESH
        )

    inputs = {KEY: k_in, VALUE: v_in, QUERY: q_in, GRAD: g_in}

    def landing(array, h):
        return kv.at[0, array, h] if array < 2 else qg.at[array - 2, h]

    def columns(e, h):
        return pl.ds(pl.multiple_of(e * 256 + h * 128, 128), 128)

    def rows_of(e):
        return pl.ds(pl.multiple_of(e * ROWS, ROWS), ROWS)

    order = [(KEY, 0), (VALUE, 0), (QUERY, 0), (KEY, 1), (VALUE, 1), (GRAD, 0), (QUERY, 1), (GRAD, 1)]

    def local_in(array, h):
        return pltpu.make_async_copy(
            inputs[array].at[:, columns(me, h)], landing(array, h).at[rows_of(me)], in_local.at[array, h]
        )

    for array, h in order:
        local_in(array, h).start()

    barrier = pltpu.get_barrier_semaphore()
    partners = [device(x, y, me ^ k) for k in range(1, 8)] + near_device + far_device
    for partner in partners:
        pl.semaphore_signal(barrier, inc=1, device_id=partner, device_id_type=MESH)
    pl.semaphore_wait(barrier, len(partners))

    def start_in(array, h, chip):
        for c in range(2):
            e = (z ^ chip) * 2 + (core ^ 1 if c == 0 else core)
            if chip or c == 0:
                remote(
                    inputs[array].at[:, columns(e, h)],
                    landing(array, h).at[rows_of(me)],
                    in_send.at[array, h],
                    in_recv.at[array, h, chip],
                    device(x, y, e),
                ).start()

    def wait_in(array, h, chip):
        rows = ROWS if chip == 0 else 2 * ROWS
        part = landing(array, h).at[pl.ds(0, rows)]
        pltpu.make_async_copy(part, part, in_recv.at[array, h, chip]).wait()

    z_hi = z // 2

    def at(i):
        return 1 - z_hi if i == 0 else z_hi

    def block_rows(s):
        return pl.ds(pl.multiple_of(s * BLOCK, BLOCK), BLOCK)

    def hop(axis, hop_at, array, h, chip):
        source = 0 if hop_at == 0 else 1 + 2 * axis
        rows = pl.ds(pl.multiple_of((z ^ chip) * 256, 256), 256)
        return remote(
            kv.at[source, array, h, rows],
            kv.at[1 + 2 * axis + hop_at, array, h, rows],
            fwd_send.at[axis, hop_at, array, h, chip],
            fwd_recv.at[axis, hop_at, array, h, chip],
            near_device[axis] if hop_at == 0 else far_device[axis],
        )

    def start_own(array, h, e):
        for axis in range(2):
            remote(
                kv.at[0, array, h, rows_of(e)],
                kv.at[1 + 2 * axis, array, h, rows_of(e)],
                fwd_send.at[axis, 0, array, h, 0],
                fwd_recv.at[axis, 0, array, h, 0],
                near_device[axis],
            ).start()

    def start_near(array, h, chip):
        wait_in(array, h, chip)
        for axis in range(2):
            hop(axis, 0, array, h, chip).start()

    def pass_on(array, h, chip):
        for axis in range(2):
            hop(axis, 0, array, h, chip).wait_recv()
            hop(axis, 1, array, h, chip).start()

    def wait_far(h, chips):
        for chip in chips:
            for array in range(2):
                for axis in range(2):
                    hop(axis, 1, array, h, chip).wait_recv()

    def turn(array, h, i):
        if i == 1:
            local_in(array, h).wait()
        for chip in (2, 3) if i == 0 else (0, 1):
            wait_in(array, h, chip)
        qg_t[array - 2, h, at(i)] = qg[array - 2, h, block_rows(at(i)), :].T

    def pair(j, h, s):
        source = 0 if j < 2 else j - 1
        rows = block_rows(1 - s if j == 1 else s)
        return kv[source, 0, h, rows, :], kv[source, 1, h, rows, :]

    def forward(group, h, i):
        s = at(i)
        pairs = [pair(j, h, s) for j in GROUPS[group]]
        scores = [dot(keys, qg_t[0, h, s], 1, 0) for keys, _ in pairs]
        peak = jnp.maximum(*[jnp.max(each, axis=0, keepdims=True) for each in scores])
        total, part = 0.0, 0.0
        for j, each, (_, values) in zip(GROUPS[group], scores, pairs):
            shifted = jnp.exp2((each - peak) * EXP2_SCALE)
            total = total + jnp.sum(shifted, axis=0, keepdims=True)
            low = shifted.astype(BF16)
            weights[h, j, s] = low
            part = part + dot(values, low, 0, 0)
        peaks[h, group, s] = peak
        if group == 0:
            run_peak[h, s] = peak
            run_total[h, s] = total
            out_acc[h, s] = part
        else:
            old = run_peak[h, s]
            joined = jnp.maximum(old, peak)
            keep = jnp.exp2((old - joined) * EXP2_SCALE)
            fresh = jnp.exp2((peak - joined) * EXP2_SCALE)
            run_peak[h, s] = joined
            run_total[h, s] = run_total[h, s] * keep + total * fresh
            out_acc[h, s] = out_acc[h, s] * keep + part * fresh

    outs = [out0, out1, out2, out3]

    def out_copy(array, h, e):
        return remote(
            staged.at[array, h, rows_of(e)],
            outs[array].at[:, columns(me, h)],
            out_send.at[array, h],
            out_recv.at[array, h],
            device(x, y, e),
        )

    def out_keep(array, h):
        return pltpu.make_async_copy(
            staged.at[array, h, rows_of(me)], outs[array].at[:, columns(me, h)], out_local.at[array, h]
        )

    def send_out(array, h, i):
        for chip in (2, 3) if i == 0 else (1, 0):
            for c in range(2):
                e = (z ^ chip) * 2 + (core ^ 1 if c == 0 else core)
                if chip or c == 0:
                    out_copy(array, h, e).start()
        if i == 1:
            out_keep(array, h).start()

    def finish_forward(h, i):
        s = at(i)
        attended = (out_acc[h, s] / run_total[h, s]).astype(BF16)
        dots[h, s] = jnp.sum(attended.astype(F32) * qg_t[1, h, s].astype(F32), axis=0, keepdims=True)
        staged[0, h, block_rows(s)] = attended.T

    def finish_queries(h, i):
        s = at(i)
        staged[1, h, block_rows(s)] = query_acc[h, s].astype(BF16).T
        send_out(1, h, i)

    def far_copy(axis, array, h, s):
        return remote(
            far_send.at[axis, array, h, s], far_recv.at[axis, array, h, s],
            far_ssem.at[axis, array, h, s], far_rsem.at[axis, array, h, s], far_device[axis],
        )

    def near_copy(axis, array, h, s):
        return remote(
            near_send.at[axis, array, h, s], near_recv.at[axis, array, h, s],
            near_ssem.at[axis, array, h, s], near_rsem.at[axis, array, h, s], near_device[axis],
        )

    def backward(group, h, i):
        s = at(i)
        factor = jnp.exp2((peaks[h, group, s] - run_peak[h, s]) * EXP2_SCALE) / run_total[h, s]
        scaled = factor * SCALE
        grads = qg_t[1, h, s]
        grads_scaled = (grads.astype(F32) * factor).astype(BF16)
        queries_scaled = (qg_t[0, h, s].astype(F32) * scaled).astype(BF16)
        query_part = 0.0
        for j in GROUPS[group]:
            axis = (j - 2) // 2
            keys, values = pair(j, h, s)
            low = weights[h, j, s]
            grad_probs = dot(values, grads, 1, 0)
            grad_scores = (low.astype(F32) * (grad_probs - dots[h, s])).astype(BF16)
            query_part = query_part + dot(keys, grad_scores, 0, 0)
            value_term = dot(low, grads_scaled, 1, 1)
            key_term = dot(grad_scores, queries_scaled, 1, 1)
            for array, term in ((0, key_term), (1, value_term)):
                if group == 2:
                    far_send[axis, array, h, s] = term.astype(BF16)
                elif group == 1:
                    near[axis, array, h, s] = term
                elif i == 1 - h:
                    acc[array, h, s if j == 0 else 1 - s] = term
                else:
                    place = s if j == 0 else 1 - s
                    acc[array, h, place] = acc[array, h, place] + term
        if group == 2:
            query_acc[h, s] = query_part * scaled
        else:
            query_acc[h, s] = query_acc[h, s] + query_part * scaled

    def send_far(h, i):
        for array in range(2):
            for axis in range(2):
                far_copy(axis, array, h, at(i)).start()

    def reduce_near(h, i, array):
        s = at(i)
        for axis in range(2):
            far_copy(axis, array, h, s).wait_recv()
            near_send[axis, array, h, s] = (
                near[axis, array, h, s] + far_recv[axis, array, h, s].astype(F32)
            ).astype(BF16)
            near_copy(axis, array, h, s).start()

    def finish_keys(h, i, array):
        s = at(i)
        total = acc[array, h, s]
        for axis in range(2):
            near_copy(axis, array, h, s).wait_recv()
            total = total + near_recv[axis, array, h, s].astype(F32)
        staged[2 + array, h, block_rows(s)] = total.astype(BF16)
        send_out(2 + array, h, i)

    first = ((KEY, 0), (VALUE, 0), (KEY, 1), (VALUE, 1))
    for array, h in first:
        start_in(array, h, 0)
    for array, h in first:
        local_in(array, h).wait()
        start_own(array, h, me)
    for chip in (1, 2, 3):
        start_in(KEY, 0, chip)
    for chip in (1, 2, 3):
        start_in(VALUE, 0, chip)
    for array, h in first:
        wait_in(array, h, 0)
        start_own(array, h, me ^ 1)
    for array, h, chips in (
        (QUERY, 0, (0, 1, 2, 3)), (GRAD, 0, (0, 1)), (KEY, 1, (2, 3, 1)), (VALUE, 1, (2, 3, 1)),
        (GRAD, 0, (2, 3)), (QUERY, 1, (2, 3, 1, 0)), (GRAD, 1, (2, 3, 1, 0)),
    ):
        for chip in chips:
            start_in(array, h, chip)

    start_near(KEY, 0, 1)
    pass_on(KEY, 0, 0)
    pass_on(VALUE, 0, 0)
    start_near(VALUE, 0, 1)
    start_near(KEY, 0, 3)
    start_near(KEY, 0, 2)
    pass_on(KEY, 1, 0)
    pass_on(VALUE, 1, 0)
    start_near(VALUE, 0, 3)
    start_near(VALUE, 0, 2)
    pass_on(KEY, 0, 1)
    turn(QUERY, 0, 1)
    pass_on(VALUE, 0, 1)
    forward(0, 0, 1)
    pass_on(KEY, 0, 3)
    forward(1, 0, 1)
    pass_on(KEY, 0, 2)
    turn(GRAD, 0, 1)
    start_near(KEY, 1, 3)
    start_near(KEY, 1, 2)
    pass_on(VALUE, 0, 3)
    wait_far(0, (0, 1))
    forward(2, 0, 1)
    pass_on(VALUE, 0, 2)
    finish_forward(0, 1)
    send_out(0, 0, 1)
    backward(2, 0, 1)
    start_near(KEY, 1, 1)
    start_near(VALUE, 1, 3)
    start_near(VALUE, 1, 2)
    pass_on(KEY, 1, 3)
    backward(1, 0, 1)
    start_near(VALUE, 1, 1)
    pass_on(KEY, 1, 2)
    backward(0, 0, 1)
    finish_queries(0, 1)
    turn(QUERY, 0, 0)
    pass_on(VALUE, 1, 3)
    forward(0, 0, 0)
    forward(1, 0, 0)
    pass_on(VALUE, 1, 2)
    wait_far(0, (3, 2))
    forward(2, 0, 0)
    turn(GRAD, 0, 0)
    finish_forward(0, 0)
    pass_on(KEY, 1, 1)
    send_far(0, 1)
    send_out(0, 0, 0)
    backward(2, 0, 0)
    pass_on(VALUE, 1, 1)
    send_far(0, 0)
    backward(1, 0, 0)
    backward(0, 0, 0)
    finish_queries(0, 0)
    turn(QUERY, 1, 1)
    turn(QUERY, 1, 0)
    forward(0, 1, 0)
    reduce_near(0, 1, 0)
    forward(1, 1, 0)
    turn(GRAD, 1, 1)
    turn(GRAD, 1, 0)
    wait_far(1, (3, 2))
    forward(2, 1, 0)
    reduce_near(0, 1, 1)
    finish_forward(1, 0)
    backward(2, 1, 0)
    send_far(1, 0)
    send_out(0, 1, 0)
    forward(0, 1, 1)
    reduce_near(0, 0, 0)
    forward(1, 1, 1)
    wait_far(1, (0, 1))
    forward(2, 1, 1)
    finish_forward(1, 1)
    backward(2, 1, 1)
    send_far(1, 1)
    reduce_near(0, 0, 1)
    send_out(0, 1, 1)
    finish_keys(0, 1, 0)
    backward(1, 1, 0)
    reduce_near(1, 0, 0)
    finish_keys(0, 1, 1)
    backward(1, 1, 1)
    reduce_near(1, 0, 1)
    finish_keys(0, 0, 0)
    backward(0, 1, 0)
    finish_queries(1, 0)
    finish_keys(0, 0, 1)
    reduce_near(1, 1, 0)
    backward(0, 1, 1)
    finish_queries(1, 1)
    finish_keys(1, 0, 0)
    reduce_near(1, 1, 1)
    finish_keys(1, 0, 1)
    finish_keys(1, 1, 0)
    finish_keys(1, 1, 1)

    for array in range(4):
        for h in range(2):
            part = landing(array, h).at[pl.ds(0, 7 * ROWS)]
            pltpu.make_async_copy(part, part, in_send.at[array, h]).wait()
    for array in range(2):
        for h in range(2):
            for axis in range(2):
                for chip in range(4):
                    hop(axis, 0, array, h, chip).wait_send()
                    hop(axis, 1, array, h, chip).wait_send()
                for s in range(2):
                    far_copy(axis, array, h, s).wait_send()
                    near_copy(axis, array, h, s).wait_send()
    for array in range(4):
        for h in range(2):
            out_keep(array, h).wait()
            part = staged.at[array, h, pl.ds(0, 7 * ROWS)]
            pltpu.make_async_copy(part, part, out_send.at[array, h]).wait()
            pltpu.make_async_copy(part, part, out_recv.at[array, h]).wait()


def keep_kernel(in0, in1, in2, in3, out0, out1, out2, out3, done):
    copies = [
        pltpu.make_async_copy(src, dst, done.at[i])
        for i, (src, dst) in enumerate(((in0, out0), (in1, out1), (in2, out2), (in3, out3)))
    ]
    for copy in copies:
        copy.start()
    for copy in copies:
        copy.wait()


def body(queries, key_rows, value_rows, grad_out):
    dma = pltpu.SemaphoreType.DMA
    term = (2, 2, 2, 2, BLOCK, HEAD_DIM)
    shape = jax.ShapeDtypeStruct(queries.shape, BF16)
    results = pl.pallas_call(
        kernel,
        out_shape=[shape] * 4,
        in_specs=[pl.BlockSpec(memory_space=pl.ANY)] * 4,
        out_specs=[pl.BlockSpec(memory_space=pl.ANY)] * 4,
        scratch_shapes=[
            pltpu.VMEM((5, 2, 2, 2 * BLOCK, HEAD_DIM), BF16),
            pltpu.VMEM((2, 2, 2 * BLOCK, HEAD_DIM), BF16),
            pltpu.VMEM((2, 2, 2, HEAD_DIM, BLOCK), BF16),
            pltpu.VMEM((2, 6, 2, BLOCK, BLOCK), BF16),
            pltpu.VMEM((2, 6, 2, 1, BLOCK), F32),
            pltpu.VMEM((2, 2, 1, BLOCK), F32),
            pltpu.VMEM((2, 2, 1, BLOCK), F32),
            pltpu.VMEM((2, 2, HEAD_DIM, BLOCK), F32),
            pltpu.VMEM((2, 2, HEAD_DIM, BLOCK), F32),
            pltpu.VMEM((2, 2, 1, BLOCK), F32),
            pltpu.VMEM((2, 2, 2, BLOCK, HEAD_DIM), F32),
            pltpu.VMEM(term, F32),
            pltpu.VMEM(term, BF16),
            pltpu.VMEM(term, BF16),
            pltpu.VMEM(term, BF16),
            pltpu.VMEM(term, BF16),
            pltpu.VMEM((4, 2, 2 * BLOCK, HEAD_DIM), BF16),
            dma((4, 2)), dma((4, 2, 4)), dma((4, 2)),
            dma((2, 2, 2, 2, 4)), dma((2, 2, 2, 2, 4)),
            dma((2, 2, 2, 2)), dma((2, 2, 2, 2)), dma((2, 2, 2, 2)), dma((2, 2, 2, 2)),
            dma((4, 2)), dma((4, 2)), dma((4, 2)),
        ],
        compiler_params=pltpu.CompilerParams(
            collective_id=0, has_side_effects=True, vmem_limit_bytes=103 * 2 ** 19
        ),
        cost_estimate=pl.CostEstimate(
            flops=7 * 24 * 2 * BLOCK * BLOCK * HEAD_DIM, bytes_accessed=2 ** 22, transcendentals=24 * BLOCK * BLOCK
        ),
        name="butterfly_attention",
    )(queries, key_rows, value_rows, grad_out)
    return pl.pallas_call(
        keep_kernel,
        out_shape=[shape] * 4,
        in_specs=[pl.BlockSpec(memory_space=pl.ANY)] * 4,
        out_specs=[pl.BlockSpec(memory_space=pl.ANY)] * 4,
        scratch_shapes=[dma((4,))],
        compiler_params=pltpu.CompilerParams(vmem_limit_bytes=2 * 2 ** 20),
        name="keep_results",
    )(*results)


def solution(mesh):
    placed = P(("context", "ulysses"), None)
    return jax.shard_map(
        body, mesh=mesh, in_specs=(placed,) * 4, out_specs=(placed,) * 4, check_vma=False
    )
```

```python
import jax
import jax.numpy as jnp
from jax import lax
from jax.experimental import pallas as pl
from jax.experimental.pallas import tpu as pltpu
from jax.sharding import PartitionSpec as P

HEAD_DIM = 128
BLOCK = 512
ROWS = 128
F32 = jnp.float32
BF16 = jnp.bfloat16
SCALE = HEAD_DIM ** -0.5
EXP2_SCALE = SCALE * 1.4426950408889634
MESH = pl.DeviceIdType.MESH

KEY, VALUE, QUERY, GRAD = range(4)
GROUPS = ((0, 1), (2, 4), (3, 5))


def dot(a, b, ca, cb):
    return lax.dot_general(a, b, (((ca,), (cb,)), ((), ())), preferred_element_type=F32)


def kernel(
    q_in, k_in, v_in, g_in, out0, out1, out2, out3,
    kv, qg, qg_t, weights, peaks, run_peak, run_total, out_acc, query_acc, dots,
    acc, near, far_send, far_recv, near_send, near_recv, staged,
    in_send, in_recv, in_local, fwd_send, fwd_recv, far_ssem, far_rsem, near_ssem, near_rsem,
    out_send, out_recv, out_local,
):
    context = lax.axis_index("context")
    ulysses = lax.axis_index("ulysses")
    x = context // 8
    y = (context // 2) % 4
    z = (context % 2) * 2 + ulysses // 2
    core = ulysses % 2
    me = z * 2 + core

    def device(x, y, e):
        return {"context": x * 8 + y * 2 + e // 4, "ulysses": e % 4}

    def near_of(v):
        return v + 1 - 2 * (v % 2)

    def far_of(v):
        return 3 - v

    near_device = [device(near_of(x), y, me), device(x, near_of(y), me)]
    far_device = [device(far_of(x), y, me), device(x, far_of(y), me)]

    def remote(src, dst, ssem, rsem, to):
        return pltpu.make_async_remote_copy(
            src_ref=src, dst_ref=dst, send_sem=ssem, recv_sem=rsem, device_id=to, device_id_type=MESH
        )

    inputs = {KEY: k_in, VALUE: v_in, QUERY: q_in, GRAD: g_in}

    def landing(array, h):
        return kv.at[0, array, h] if array < 2 else qg.at[array - 2, h]

    def columns(e, h):
        return pl.ds(pl.multiple_of(e * 256 + h * 128, 128), 128)

    def rows_of(e):
        return pl.ds(pl.multiple_of(e * ROWS, ROWS), ROWS)

    order = [(KEY, 0), (VALUE, 0), (QUERY, 0), (KEY, 1), (VALUE, 1), (GRAD, 0), (QUERY, 1), (GRAD, 1)]

    def local_in(array, h):
        return pltpu.make_async_copy(
            inputs[array].at[:, columns(me, h)], landing(array, h).at[rows_of(me)], in_local.at[array, h]
        )

    for array, h in order:
        local_in(array, h).start()

    barrier = pltpu.get_barrier_semaphore()
    partners = [device(x, y, me ^ k) for k in range(1, 8)] + near_device + far_device
    for partner in partners:
        pl.semaphore_signal(barrier, inc=1, device_id=partner, device_id_type=MESH)
    pl.semaphore_wait(barrier, len(partners))

    def start_in(array, h, chip):
        for c in range(2):
            e = (z ^ chip) * 2 + (core ^ 1 if c == 0 else core)
            if chip or c == 0:
                remote(
                    inputs[array].at[:, columns(e, h)],
                    landing(array, h).at[rows_of(me)],
                    in_send.at[array, h],
                    in_recv.at[array, h, chip],
                    device(x, y, e),
                ).start()

    def wait_in(array, h, chip):
        rows = ROWS if chip == 0 else 2 * ROWS
        part = landing(array, h).at[pl.ds(0, rows)]
        pltpu.make_async_copy(part, part, in_recv.at[array, h, chip]).wait()

    z_hi = z // 2

    def at(i):
        return 1 - z_hi if i == 0 else z_hi

    def block_rows(s):
        return pl.ds(pl.multiple_of(s * BLOCK, BLOCK), BLOCK)

    def hop(axis, hop_at, array, h, chip):
        source = 0 if hop_at == 0 else 1 + 2 * axis
        rows = pl.ds(pl.multiple_of((z ^ chip) * 256, 256), 256)
        return remote(
            kv.at[source, array, h, rows],
            kv.at[1 + 2 * axis + hop_at, array, h, rows],
            fwd_send.at[axis, hop_at, array, h, chip],
            fwd_recv.at[axis, hop_at, array, h, chip],
            near_device[axis] if hop_at == 0 else far_device[axis],
        )

    def start_own(array, h, e):
        for axis in range(2):
            remote(
                kv.at[0, array, h, rows_of(e)],
                kv.at[1 + 2 * axis, array, h, rows_of(e)],
                fwd_send.at[axis, 0, array, h, 0],
                fwd_recv.at[axis, 0, array, h, 0],
                near_device[axis],
            ).start()

    def start_near(array, h, chip):
        wait_in(array, h, chip)
        for axis in range(2):
            hop(axis, 0, array, h, chip).start()

    def pass_on(array, h, chip):
        for axis in range(2):
            hop(axis, 0, array, h, chip).wait_recv()
            hop(axis, 1, array, h, chip).start()

    def wait_far(h, chips):
        for chip in chips:
            for array in range(2):
                for axis in range(2):
                    hop(axis, 1, array, h, chip).wait_recv()

    def turn(array, h, i):
        if i == 1:
            local_in(array, h).wait()
        for chip in (2, 3) if i == 0 else (0, 1):
            wait_in(array, h, chip)
        qg_t[array - 2, h, at(i)] = qg[array - 2, h, block_rows(at(i)), :].T

    def pair(j, h, s):
        source = 0 if j < 2 else j - 1
        rows = block_rows(1 - s if j == 1 else s)
        return kv[source, 0, h, rows, :], kv[source, 1, h, rows, :]

    def forward(group, h, i):
        s = at(i)
        pairs = [pair(j, h, s) for j in GROUPS[group]]
        scores = [dot(keys, qg_t[0, h, s], 1, 0) for keys, _ in pairs]
        peak = jnp.maximum(*[jnp.max(each, axis=0, keepdims=True) for each in scores])
        total, part = 0.0, 0.0
        for j, each, (_, values) in zip(GROUPS[group], scores, pairs):
            shifted = jnp.exp2((each - peak) * EXP2_SCALE)
            total = total + jnp.sum(shifted, axis=0, keepdims=True)
            low = shifted.astype(BF16)
            weights[h, j, s] = low
            part = part + dot(values, low, 0, 0)
        peaks[h, group, s] = peak
        if group == 0:
            run_peak[h, s] = peak
            run_total[h, s] = total
            out_acc[h, s] = part
        else:
            old = run_peak[h, s]
            joined = jnp.maximum(old, peak)
            keep = jnp.exp2((old - joined) * EXP2_SCALE)
            fresh = jnp.exp2((peak - joined) * EXP2_SCALE)
            run_peak[h, s] = joined
            run_total[h, s] = run_total[h, s] * keep + total * fresh
            out_acc[h, s] = out_acc[h, s] * keep + part * fresh

    outs = [out0, out1, out2, out3]

    def out_copy(array, h, e):
        return remote(
            staged.at[array, h, rows_of(e)],
            outs[array].at[:, columns(me, h)],
            out_send.at[array, h],
            out_recv.at[array, h],
            device(x, y, e),
        )

    def out_keep(array, h):
        return pltpu.make_async_copy(
            staged.at[array, h, rows_of(me)], outs[array].at[:, columns(me, h)], out_local.at[array, h]
        )

    def send_out(array, h, i):
        for chip in (2, 3) if i == 0 else (1, 0):
            for c in range(2):
                e = (z ^ chip) * 2 + (core ^ 1 if c == 0 else core)
                if chip or c == 0:
                    out_copy(array, h, e).start()
        if i == 1:
            out_keep(array, h).start()

    def finish_forward(h, i):
        s = at(i)
        attended = (out_acc[h, s] / run_total[h, s]).astype(BF16)
        dots[h, s] = jnp.sum(attended.astype(F32) * qg_t[1, h, s].astype(F32), axis=0, keepdims=True)
        staged[0, h, block_rows(s)] = attended.T

    def finish_queries(h, i):
        s = at(i)
        staged[1, h, block_rows(s)] = query_acc[h, s].astype(BF16).T
        send_out(1, h, i)

    def far_copy(axis, array, h, s):
        return remote(
            far_send.at[axis, array, h, s], far_recv.at[axis, array, h, s],
            far_ssem.at[axis, array, h, s], far_rsem.at[axis, array, h, s], far_device[axis],
        )

    def near_copy(axis, array, h, s):
        return remote(
            near_send.at[axis, array, h, s], near_recv.at[axis, array, h, s],
            near_ssem.at[axis, array, h, s], near_rsem.at[axis, array, h, s], near_device[axis],
        )

    def backward(group, h, i):
        s = at(i)
        factor = jnp.exp2((peaks[h, group, s] - run_peak[h, s]) * EXP2_SCALE) / run_total[h, s]
        scaled = factor * SCALE
        grads = qg_t[1, h, s]
        grads_scaled = (grads.astype(F32) * factor).astype(BF16)
        queries_scaled = (qg_t[0, h, s].astype(F32) * scaled).astype(BF16)
        query_part = 0.0
        for j in GROUPS[group]:
            axis = (j - 2) // 2
            keys, values = pair(j, h, s)
            low = weights[h, j, s]
            grad_probs = dot(values, grads, 1, 0)
            grad_scores = (low.astype(F32) * (grad_probs - dots[h, s])).astype(BF16)
            query_part = query_part + dot(keys, grad_scores, 0, 0)
            value_term = dot(low, grads_scaled, 1, 1)
            key_term = dot(grad_scores, queries_scaled, 1, 1)
            for array, term in ((0, key_term), (1, value_term)):
                if group == 2:
                    far_send[axis, array, h, s] = term.astype(BF16)
                elif group == 1:
                    near[axis, array, h, s] = term
                elif i == 1 - h:
                    acc[array, h, s if j == 0 else 1 - s] = term
                else:
                    place = s if j == 0 else 1 - s
                    acc[array, h, place] = acc[array, h, place] + term
        if group == 2:
            query_acc[h, s] = query_part * scaled
        else:
            query_acc[h, s] = query_acc[h, s] + query_part * scaled

    def send_far(h, i):
        for array in range(2):
            for axis in range(2):
                far_copy(axis, array, h, at(i)).start()

    def reduce_near(h, i, array):
        s = at(i)
        for axis in range(2):
            far_copy(axis, array, h, s).wait_recv()
            near_send[axis, array, h, s] = (
                near[axis, array, h, s] + far_recv[axis, array, h, s].astype(F32)
            ).astype(BF16)
            near_copy(axis, array, h, s).start()

    def finish_keys(h, i, array):
        s = at(i)
        total = acc[array, h, s]
        for axis in range(2):
            near_copy(axis, array, h, s).wait_recv()
            total = total + near_recv[axis, array, h, s].astype(F32)
        staged[2 + array, h, block_rows(s)] = total.astype(BF16)
        send_out(2 + array, h, i)

    first = ((KEY, 0), (VALUE, 0), (KEY, 1), (VALUE, 1))
    for array, h in first:
        start_in(array, h, 0)
    for array, h in first:
        local_in(array, h).wait()
        start_own(array, h, me)
    for chip in (1, 2, 3):
        start_in(KEY, 0, chip)
    for chip in (1, 2, 3):
        start_in(VALUE, 0, chip)
    for array, h in first:
        wait_in(array, h, 0)
        start_own(array, h, me ^ 1)
    for array, h, chips in (
        (QUERY, 0, (0, 1, 2, 3)), (GRAD, 0, (0, 1)), (KEY, 1, (2, 3, 1)), (VALUE, 1, (2, 3, 1)),
        (GRAD, 0, (2, 3)), (QUERY, 1, (2, 3, 1, 0)), (GRAD, 1, (2, 3, 1, 0)),
    ):
        for chip in chips:
            start_in(array, h, chip)

    start_near(KEY, 0, 1)
    pass_on(KEY, 0, 0)
    pass_on(VALUE, 0, 0)
    start_near(VALUE, 0, 1)
    start_near(KEY, 0, 3)
    start_near(KEY, 0, 2)
    pass_on(KEY, 1, 0)
    pass_on(VALUE, 1, 0)
    start_near(VALUE, 0, 3)
    start_near(VALUE, 0, 2)
    pass_on(KEY, 0, 1)
    turn(QUERY, 0, 1)
    pass_on(VALUE, 0, 1)
    forward(0, 0, 1)
    pass_on(KEY, 0, 3)
    forward(1, 0, 1)
    pass_on(KEY, 0, 2)
    turn(GRAD, 0, 1)
    start_near(KEY, 1, 3)
    start_near(KEY, 1, 2)
    pass_on(VALUE, 0, 3)
    wait_far(0, (0, 1))
    forward(2, 0, 1)
    pass_on(VALUE, 0, 2)
    finish_forward(0, 1)
    send_out(0, 0, 1)
    backward(2, 0, 1)
    start_near(KEY, 1, 1)
    start_near(VALUE, 1, 3)
    start_near(VALUE, 1, 2)
    pass_on(KEY, 1, 3)
    backward(1, 0, 1)
    start_near(VALUE, 1, 1)
    pass_on(KEY, 1, 2)
    backward(0, 0, 1)
    finish_queries(0, 1)
    turn(QUERY, 0, 0)
    pass_on(VALUE, 1, 3)
    forward(0, 0, 0)
    forward(1, 0, 0)
    pass_on(VALUE, 1, 2)
    wait_far(0, (3, 2))
    forward(2, 0, 0)
    turn(GRAD, 0, 0)
    finish_forward(0, 0)
    pass_on(KEY, 1, 1)
    send_far(0, 1)
    send_out(0, 0, 0)
    backward(2, 0, 0)
    pass_on(VALUE, 1, 1)
    send_far(0, 0)
    backward(1, 0, 0)
    backward(0, 0, 0)
    finish_queries(0, 0)
    turn(QUERY, 1, 1)
    turn(QUERY, 1, 0)
    forward(0, 1, 0)
    reduce_near(0, 1, 0)
    forward(1, 1, 0)
    turn(GRAD, 1, 1)
    turn(GRAD, 1, 0)
    wait_far(1, (3, 2))
    forward(2, 1, 0)
    reduce_near(0, 1, 1)
    finish_forward(1, 0)
    backward(2, 1, 0)
    send_far(1, 0)
    send_out(0, 1, 0)
    forward(0, 1, 1)
    reduce_near(0, 0, 0)
    forward(1, 1, 1)
    wait_far(1, (0, 1))
    forward(2, 1, 1)
    finish_forward(1, 1)
    backward(2, 1, 1)
    send_far(1, 1)
    reduce_near(0, 0, 1)
    send_out(0, 1, 1)
    finish_keys(0, 1, 0)
    backward(1, 1, 0)
    reduce_near(1, 0, 0)
    finish_keys(0, 1, 1)
    backward(0, 1, 0)
    finish_queries(1, 0)
    reduce_near(1, 0, 1)
    finish_keys(0, 0, 0)
    backward(1, 1, 1)
    finish_keys(0, 0, 1)
    reduce_near(1, 1, 0)
    backward(0, 1, 1)
    finish_queries(1, 1)
    finish_keys(1, 0, 0)
    reduce_near(1, 1, 1)
    finish_keys(1, 0, 1)
    finish_keys(1, 1, 0)
    finish_keys(1, 1, 1)

    for array in range(4):
        for h in range(2):
            part = landing(array, h).at[pl.ds(0, 7 * ROWS)]
            pltpu.make_async_copy(part, part, in_send.at[array, h]).wait()
    for array in range(2):
        for h in range(2):
            for axis in range(2):
                for chip in range(4):
                    hop(axis, 0, array, h, chip).wait_send()
                    hop(axis, 1, array, h, chip).wait_send()
                for s in range(2):
                    far_copy(axis, array, h, s).wait_send()
                    near_copy(axis, array, h, s).wait_send()
    for array in range(4):
        for h in range(2):
            out_keep(array, h).wait()
            part = staged.at[array, h, pl.ds(0, 7 * ROWS)]
            pltpu.make_async_copy(part, part, out_send.at[array, h]).wait()
            pltpu.make_async_copy(part, part, out_recv.at[array, h]).wait()


def keep_kernel(in0, in1, in2, in3, out0, out1, out2, out3, done):
    copies = [
        pltpu.make_async_copy(src, dst, done.at[i])
        for i, (src, dst) in enumerate(((in0, out0), (in1, out1), (in2, out2), (in3, out3)))
    ]
    for copy in copies:
        copy.start()
    for copy in copies:
        copy.wait()


def body(queries, key_rows, value_rows, grad_out):
    dma = pltpu.SemaphoreType.DMA
    term = (2, 2, 2, 2, BLOCK, HEAD_DIM)
    shape = jax.ShapeDtypeStruct(queries.shape, BF16)
    results = pl.pallas_call(
        kernel,
        out_shape=[shape] * 4,
        in_specs=[pl.BlockSpec(memory_space=pl.ANY)] * 4,
        out_specs=[pl.BlockSpec(memory_space=pl.ANY)] * 4,
        scratch_shapes=[
            pltpu.VMEM((5, 2, 2, 2 * BLOCK, HEAD_DIM), BF16),
            pltpu.VMEM((2, 2, 2 * BLOCK, HEAD_DIM), BF16),
            pltpu.VMEM((2, 2, 2, HEAD_DIM, BLOCK), BF16),
            pltpu.VMEM((2, 6, 2, BLOCK, BLOCK), BF16),
            pltpu.VMEM((2, 6, 2, 1, BLOCK), F32),
            pltpu.VMEM((2, 2, 1, BLOCK), F32),
            pltpu.VMEM((2, 2, 1, BLOCK), F32),
            pltpu.VMEM((2, 2, HEAD_DIM, BLOCK), F32),
            pltpu.VMEM((2, 2, HEAD_DIM, BLOCK), F32),
            pltpu.VMEM((2, 2, 1, BLOCK), F32),
            pltpu.VMEM((2, 2, 2, BLOCK, HEAD_DIM), F32),
            pltpu.VMEM(term, F32),
            pltpu.VMEM(term, BF16),
            pltpu.VMEM(term, BF16),
            pltpu.VMEM(term, BF16),
            pltpu.VMEM(term, BF16),
            pltpu.VMEM((4, 2, 2 * BLOCK, HEAD_DIM), BF16),
            dma((4, 2)), dma((4, 2, 4)), dma((4, 2)),
            dma((2, 2, 2, 2, 4)), dma((2, 2, 2, 2, 4)),
            dma((2, 2, 2, 2)), dma((2, 2, 2, 2)), dma((2, 2, 2, 2)), dma((2, 2, 2, 2)),
            dma((4, 2)), dma((4, 2)), dma((4, 2)),
        ],
        compiler_params=pltpu.CompilerParams(
            collective_id=0, has_side_effects=True, vmem_limit_bytes=103 * 2 ** 19
        ),
        cost_estimate=pl.CostEstimate(
            flops=7 * 24 * 2 * BLOCK * BLOCK * HEAD_DIM, bytes_accessed=2 ** 22, transcendentals=24 * BLOCK * BLOCK
        ),
        name="butterfly_attention",
    )(queries, key_rows, value_rows, grad_out)
    return pl.pallas_call(
        keep_kernel,
        out_shape=[shape] * 4,
        in_specs=[pl.BlockSpec(memory_space=pl.ANY)] * 4,
        out_specs=[pl.BlockSpec(memory_space=pl.ANY)] * 4,
        scratch_shapes=[dma((4,))],
        compiler_params=pltpu.CompilerParams(vmem_limit_bytes=2 * 2 ** 20),
        name="keep_results",
    )(*results)


def solution(mesh):
    placed = P(("context", "ulysses"), None)
    return jax.shard_map(
        body, mesh=mesh, in_specs=(placed,) * 4, out_specs=(placed,) * 4, check_vma=False
    )
```
